128 devices in a mesh: half: 2 (over z_hi), row: 8 (over x, core), col: 8 (over z_lo, y).
Axes of the slice: x: 4, y: 4, z: 4 (z_hi: 2, z_lo: 2; z = z_hi * 2 + z_lo), core: 2. Of those that a mesh axis runs over, the one named last changes fastest.
Arguments:
- front: bfloat16 [2, 16384, 16384], P('half', 'row', 'col'), may hold values from -6 to 6, as said below
- panel: bfloat16 [2, 16384, 1024], P('half', 'row', 'col'), may hold values from -2.5 to 2.5
- inverse_block: bfloat16 [2, 1024, 1024], P('half', None, 'col'), as said below
- child_maps: int32 [2, 16384], replicated, may hold values from 0 to 16383, as said below
- root_front: bfloat16 [16384, 16384], P(('half', 'row'), 'col'), may hold values from -6 to 6, as said below
Outputs:
- root_sum: float32 [16384, 16384], P(('half', 'row'), 'col')
The draws below stay inside these ranges and needn't reach their ends.
Inputs may be any that keep to these rules, and one draw needn't show every extreme that they name: `child_maps`: each row is a permutation of the 16384 root indices. For each child, in every aligned block of 2048 positions, the k-th aligned run of 128 positions maps into the k-th aligned block of 1024 root indices. `inverse_block`: each matrix is lower triangular with a positive diagonal. `front`: each child's matrix is symmetric. `root_front`: the matrix is symmetric.
All inputs are finite; a program needn't handle non-finite values.
Results may differ from the reference program's by a relative error of at most 0.0041.
Values may be sent and summed in bfloat16 or wider, within the bound.
No kernel may reach another device: no remote copies, remote signals or barrier semaphores. Data moves between devices by JAX's collectives and lax.ppermute only.
A program may use at most 128 MiB of HBM per device.

```python
import jax
import jax.numpy as jnp

S = 16384
P_SIZE = 1024
CHILD_BLOCK = 2048
ROOT_BLOCK = 1024
SHARE = 128


def symmetric_field(key, shape):
    base = jax.random.normal(key, shape, jnp.float32)
    mixed = (base + jnp.swapaxes(base, -1, -2)) * 0.70710678
    return jnp.clip(mixed, -6.0, 6.0)


def draw_front(key, part):
    key = jax.random.fold_in(key, 23)
    return symmetric_field(key, (2, S, S)).astype(jnp.bfloat16)


def draw_root_front(key, part):
    key = jax.random.fold_in(key, 31)
    return symmetric_field(key, (S, S)).astype(jnp.bfloat16)


def draw_inverse_block(key, part):
    key = jax.random.fold_in(key, 11)
    first_key, second_key = jax.random.split(key)
    spread = jax.random.normal(first_key, (2, P_SIZE, P_SIZE), jnp.float32) * (0.6 / P_SIZE ** 0.5)
    diagonal = jnp.exp(jax.random.uniform(second_key, (2, P_SIZE), jnp.float32, -0.7, 0.7))
    matrix = jnp.tril(spread, -1) + diagonal[:, :, None] * jnp.eye(P_SIZE, dtype=jnp.float32)[None]
    return matrix.astype(jnp.bfloat16)


def one_map(key):
    groups = CHILD_BLOCK // SHARE
    blocks = S // CHILD_BLOCK
    within = jax.vmap(lambda subkey: jax.random.permutation(subkey, ROOT_BLOCK))(jax.random.split(key, groups))
    position = jnp.arange(CHILD_BLOCK, dtype=jnp.int32)[None, :]
    target = jnp.broadcast_to(position // SHARE, (blocks, CHILD_BLOCK))
    member = jnp.arange(blocks, dtype=jnp.int32)[:, None] * SHARE + position % SHARE
    return (target * ROOT_BLOCK + within[target, member]).reshape(-1).astype(jnp.int32)


def draw_child_maps(key, part):
    key = jax.random.fold_in(key, 5)
    return jnp.stack([one_map(jax.random.fold_in(key, 0)), one_map(jax.random.fold_in(key, 1))])


def shard_levels(rng, dims, cuts, least, high):
    gain, own = 1.0, jax.random.fold_in(rng, 6)
    for dim, parts in cuts:
        steps = jnp.exp(jax.random.uniform(jax.random.fold_in(own, dim), (parts,), jnp.float32, least / len(cuts), high / len(cuts)))
        gain = gain * jnp.repeat(steps, dims[dim] // parts).reshape([-1 if axis == dim else 1 for axis in range(len(dims))])
    return gain


def centred(key, shape, width, most, shards=(), kind=jnp.bfloat16):
    values = width * jax.random.normal(key, shape, jnp.float32)
    if shards:
        values = values * shard_levels(key, shape, shards, -0.22, 0.18)
    return jnp.clip(values, -most, most).astype(kind)


def setup_inputs(seed: int = 0) -> dict:
    key_list = jax.random.split(jax.random.key(seed), 6)
    front = draw_front(jax.random.fold_in(key_list[5], 71), 0)
    panel = centred(key_list[1], (2, S, P_SIZE), 0.18, 2.5, ((0, 2), (1, 8), (2, 8)))
    inverse_block = draw_inverse_block(jax.random.fold_in(key_list[5], 71), 0)
    child_maps = draw_child_maps(jax.random.fold_in(key_list[5], 71), 0)
    root_front = draw_root_front(jax.random.fold_in(key_list[5], 71), 0)
    return {"front": front, "panel": panel, "inverse_block": inverse_block, "child_maps": child_maps, "root_front": root_front}


def reference(front, panel, inverse_block, child_maps, root_front):
    root_sum = root_front.astype(jnp.float32)
    for child_idx in range(2):
        lower_panel = jnp.dot(panel[child_idx], inverse_block[child_idx].T, preferred_element_type=jnp.float32).astype(jnp.bfloat16)
        product = jnp.dot(lower_panel, lower_panel.T, preferred_element_type=jnp.float32)
        schur_block = (front[child_idx].astype(jnp.float32) - product).astype(jnp.bfloat16)
        inverse_map = jnp.zeros((S,), jnp.int32).at[child_maps[child_idx]].set(jnp.arange(S, dtype=jnp.int32))
        placed = jnp.take(jnp.take(schur_block, inverse_map, axis=0), inverse_map, axis=1)
        root_sum = root_sum + placed.astype(jnp.float32)
    row_ids = jnp.arange(S, dtype=jnp.int32)[:, None]
    col_ids = jnp.arange(S, dtype=jnp.int32)[None, :]
    return jnp.where(row_ids >= col_ids, root_sum, jnp.zeros_like(root_sum))
```

```python
import functools

import jax
import jax.numpy as jnp
from jax import lax
from jax.experimental import pallas as pl
from jax.experimental.pallas import tpu as pltpu
from jax.sharding import PartitionSpec as P

ALL = ("half", "row", "col")
BF16 = jnp.bfloat16
F32 = jnp.float32
VMEM_LIMIT = 58 * 1024 * 1024


def device_pairs(move):
    pairs = []
    for half in range(2):
        for row in range(8):
            for col in range(8):
                zh, x, core, zl, y = move(half, row // 2, row % 2, col // 4, col % 4)
                source = (half * 8 + row) * 8 + col
                pairs.append((source, (zh * 8 + 2 * x + core) * 8 + 4 * zl + y))
    return pairs


def shift(array, move):
    return lax.ppermute(array, ALL, device_pairs(move))


def ring(array, forward, backward):
    behind = shift(array, forward)
    ahead = shift(array, backward)
    far_first = shift(behind[0], forward)
    far_second = shift(ahead[1], backward)
    return array, behind, ahead, far_first, far_second


def lower_kernel(core_ref, panel_ref, mine_ref, other_ref, out_ref):
    core = core_ref[0]
    wide = mine_ref.shape[1]
    for ref, part in ((mine_ref, core), (other_ref, 1 - core)):
        total = jnp.zeros((panel_ref.shape[1], wide), F32)
        for chunk in range(panel_ref.shape[0]):
            total += lax.dot_general(
                panel_ref[chunk],
                ref[chunk],
                (((1,), (1,)), ((), ())),
                preferred_element_type=F32,
            )
        out_ref[:, pl.ds(pl.multiple_of(part * wide, wide), wide)] = total.astype(BF16)


def lower_piece(core, panel, mine, other):
    whole = pl.BlockSpec(memory_space=pltpu.VMEM)
    return pl.pallas_call(
        lower_kernel,
        out_shape=jax.ShapeDtypeStruct((panel.shape[1], 2 * mine.shape[1]), BF16),
        in_specs=[pl.BlockSpec(memory_space=pltpu.SMEM), whole, whole, whole],
        out_specs=whole,
        compiler_params=pltpu.CompilerParams(vmem_limit_bytes=VMEM_LIMIT),
        cost_estimate=pl.CostEstimate(
            flops=2 * 256 * 1024 * 1024, bytes_accessed=3 << 20, transcendentals=0
        ),
        name="lower",
    )(core, panel, mine, other)


def update_kernel(place_ref, *refs):
    rows, mine, other = refs[0:5], refs[5:10], refs[10:15]
    out_ref, left_ref, right_ref = refs[15:18]
    child = pl.program_id(0)
    x, core, y = place_ref[0], place_ref[1], place_ref[2]

    def gather(refs, base, store):
        near, behind, ahead, far_first, far_second = refs
        store(base, near[child])
        store((base + 3) % 4, behind[child])
        store((base + 1) % 4, ahead[child])

        @pl.when(child == 0)
        def _():
            store((base + 2) % 4, far_first[...])

        @pl.when(child == 1)
        def _():
            store((base + 2) % 4, far_second[...])

    def store_rows(at, value):
        left_ref[pl.ds(pl.multiple_of(at * 256, 256), 256), :] = value

    def store_cols(which):
        def store(at, value):
            block = (at * 2 + which) * 128
            for b in range(2):
                right_ref[b, pl.ds(pl.multiple_of(block, 128), 128), :] = value[
                    b * 128 : (b + 1) * 128
                ]

        return store

    gather(rows, y, store_rows)
    gather(mine, x, store_cols(core))
    gather(other, x, store_cols(1 - core))
    for b in range(2):
        for part in range(4):
            span = slice(part * 256, (part + 1) * 256)
            out_ref[0, b, span, :] = lax.dot_general(
                left_ref[span, :],
                right_ref[b],
                (((1,), (1,)), ((), ())),
                preferred_element_type=F32,
            )


def update(place, rows, mine, other):
    whole = pl.BlockSpec(memory_space=pltpu.VMEM)
    return pl.pallas_call(
        update_kernel,
        grid=(2,),
        out_shape=jax.ShapeDtypeStruct((2, 2, 1024, 1024), F32),
        in_specs=[pl.BlockSpec(memory_space=pltpu.SMEM)] + [whole] * 15,
        out_specs=pl.BlockSpec((1, 2, 1024, 1024), lambda c: (c, 0, 0, 0)),
        scratch_shapes=[
            pltpu.VMEM((1024, 1024), BF16),
            pltpu.VMEM((2, 1024, 1024), BF16),
        ],
        compiler_params=pltpu.CompilerParams(vmem_limit_bytes=VMEM_LIMIT),
        cost_estimate=pl.CostEstimate(
            flops=2 * 4 << 30, bytes_accessed=28 << 20, transcendentals=0
        ),
        name="update",
    )(place, *rows, *mine, *other)


ROWS_STEP = 256


def place_kernel(
    flip,
    last,
    place_ref,
    front_ref,
    update_ref,
    row_map_ref,
    col_map_ref,
    base_ref,
    out_ref,
    schur_ref,
    pick_ref,
):
    b, step = pl.program_id(0), pl.program_id(1)

    @pl.when(step == 0)
    def _():
        for r in range(8):
            for c in range(8):
                rows, cols = slice(r * 128, (r + 1) * 128), slice(c * 128, (c + 1) * 128)
                entry = front_ref[r * 8 + (c ^ flip)].astype(F32)
                schur_ref[rows, cols] = (entry - update_ref[0, 0, rows, cols]).astype(BF16)
        ids = lax.broadcasted_iota(jnp.int32, (1024, 1024), 1)
        pick_ref[...] = jnp.where(col_map_ref[0] == ids, 1.0, 0.0).astype(BF16)

    first = step * ROWS_STEP
    ids = lax.broadcasted_iota(jnp.int32, (ROWS_STEP, 1024), 0) + first
    row_pick = jnp.where(row_map_ref[...] == ids, 1.0, 0.0).astype(BF16)
    rowed = jnp.dot(row_pick, schur_ref[...], preferred_element_type=F32).astype(BF16)
    placed = jnp.dot(rowed, pick_ref[...], preferred_element_type=F32)
    total = base_ref[...].astype(F32) + placed
    if last:
        shape = (ROWS_STEP, 1024)
        row_ids = lax.broadcasted_iota(jnp.int32, shape, 0) + (place_ref[3] * 1024 + first)
        col_ids = lax.broadcasted_iota(jnp.int32, shape, 1) + (
            place_ref[4] * 2048 + b * 1024
        )
        total = jnp.where(row_ids >= col_ids, total, 0.0)
    out_ref[...] = total


def place_child(place, child, front, updates, row_map, col_map, base, flip, last):
    grid_spec = pltpu.PrefetchScalarGridSpec(
        num_scalar_prefetch=1,
        grid=(2, 1024 // ROWS_STEP),
        in_specs=[
            pl.BlockSpec((64, 128, 128), lambda b, i, s: (0, 0, b)),
            pl.BlockSpec((1, 1, 1024, 1024), lambda b, i, s: (s[child], b, 0, 0)),
            pl.BlockSpec((1, 1024), lambda b, i, s: (0, 0)),
            pl.BlockSpec((1, 1024, 1), lambda b, i, s: (b, 0, 0)),
            pl.BlockSpec((ROWS_STEP, 1024), lambda b, i, s: (i, b)),
        ],
        out_specs=pl.BlockSpec((ROWS_STEP, 1024), lambda b, i, s: (i, b)),
        scratch_shapes=[
            pltpu.VMEM((1024, 1024), BF16),
            pltpu.VMEM((1024, 1024), BF16),
        ],
    )
    return pl.pallas_call(
        functools.partial(place_kernel, flip, last),
        grid_spec=grid_spec,
        out_shape=jax.ShapeDtypeStruct((1024, 2048), F32),
        compiler_params=pltpu.CompilerParams(vmem_limit_bytes=VMEM_LIMIT),
        cost_estimate=pl.CostEstimate(
            flops=2 * 4 << 30, bytes_accessed=28 << 20, transcendentals=0
        ),
        name="place_last" if last else "place_first",
    )(place, front, updates, row_map, col_map, base)


def body(front, panel, inverse_block, child_maps, root_front):
    half = lax.axis_index("half")
    row = lax.axis_index("row")
    col = lax.axis_index("col")
    x, core, zl, y = row // 2, row % 2, col // 4, col % 4
    target = half * 8 + row

    parcels = front[0].reshape(2, 8, 128, 8, 256).transpose(0, 1, 3, 2, 4)
    stay = lax.dynamic_index_in_dim(parcels, half, 0, keepdims=False).reshape(64, 128, 256)
    leave = lax.dynamic_index_in_dim(parcels, 1 - half, 0, keepdims=False).reshape(
        64, 128, 256
    )
    crossed = shift(leave, lambda zh, x, k, zl, y: (1 - zh, x, k, 1 - zl, y))

    inverse_share = lax.dynamic_slice_in_dim(inverse_block[0], core * 512, 512, 0)
    packet = jnp.concatenate(
        [panel[0].reshape(8, 256, 128), jnp.broadcast_to(inverse_share, (8, 512, 128))], 1
    )
    packet = lax.all_to_all(packet, "col", 0, 0, tiled=True)
    own_inverse = packet[:, 256:]
    other_inverse = shift(own_inverse, lambda zh, x, k, zl, y: (zh, x, 1 - k, zl, y))
    piece = lower_piece(core.reshape(1), packet[:, :256], own_inverse, other_inverse)

    def ordered(first, second, swapped):
        return jnp.stack(
            [jnp.where(swapped, second, first), jnp.where(swapped, first, second)]
        )

    twin = shift(piece, lambda zh, x, k, zl, y: (1 - zh, x, k, zl, y))
    columns = ring(
        ordered(piece, twin, half == 1),
        lambda zh, x, k, zl, y: (zh, (x + 1) % 4, k, zl, y),
        lambda zh, x, k, zl, y: (zh, (x + 3) % 4, k, zl, y),
    )
    columns_other = [
        shift(part, lambda zh, x, k, zl, y: (zh, x, 1 - k, zl, y)) for part in columns
    ]

    same = shift(
        lax.dynamic_slice_in_dim(piece, core * 128, 128, 0),
        lambda zh, x, k, zl, y: (zl, y, k, zh, x),
    )
    cross = shift(
        lax.dynamic_slice_in_dim(piece, (1 - core) * 128, 128, 0),
        lambda zh, x, k, zl, y: (zl, y, 1 - k, zh, x),
    )
    strip = ordered(same, cross, core == 1).reshape(256, 1024)
    strip_twin = shift(strip, lambda zh, x, k, zl, y: (zh, x, k, 1 - zl, y))
    rows = ring(
        ordered(strip, strip_twin, zl == 1),
        lambda zh, x, k, zl, y: (zh, x, k, zl, (y + 1) % 4),
        lambda zh, x, k, zl, y: (zh, x, k, zl, (y + 3) % 4),
    )

    place = jnp.stack([x, core, y, target, col, half, 1 - half]).astype(jnp.int32)
    updates = update(place, rows, columns, columns_other)

    stayed = lax.all_to_all(stay, ("row", "col"), 0, 0, tiled=True)
    arrived = lax.all_to_all(crossed, ("row", "col"), 0, 0, tiled=True)

    maps = child_maps.reshape(2, 8, 16, 128)
    row_maps = (
        lax.dynamic_index_in_dim(maps, target, 2, keepdims=False).reshape(2, 1, 1024)
        - target * 1024
    )
    col_maps = lax.dynamic_slice_in_dim(maps, 2 * col, 2, 2).transpose(0, 2, 1, 3)
    col_maps = col_maps - (2 * col + jnp.arange(2, dtype=jnp.int32))[None, :, None, None] * 1024
    col_maps = col_maps.reshape(2, 2, 1024, 1)

    def pick(array, which):
        return lax.dynamic_index_in_dim(array, which, 0, keepdims=False)

    summed = place_child(
        place,
        5,
        stayed,
        updates,
        pick(row_maps, half),
        pick(col_maps, half),
        root_front,
        0,
        False,
    )
    return place_child(
        place,
        6,
        arrived,
        updates,
        pick(row_maps, 1 - half),
        pick(col_maps, 1 - half),
        summed,
        4,
        True,
    )


def solution(mesh):
    return jax.shard_map(
        body,
        mesh=mesh,
        in_specs=(
            P("half", "row", "col"),
            P("half", "row", "col"),
            P("half", None, "col"),
            P(),
            P(("half", "row"), "col"),
        ),
        out_specs=P(("half", "row"), "col"),
        check_vma=False,
    )
```

```python
import functools

import jax
import jax.numpy as jnp
from jax import lax
from jax.experimental import pallas as pl
from jax.experimental.pallas import tpu as pltpu
from jax.sharding import PartitionSpec as P

ALL = ("half", "row", "col")
BF16 = jnp.bfloat16
F32 = jnp.float32
VMEM_LIMIT = 58 * 1024 * 1024


def device_pairs(move):
    pairs = []
    for half in range(2):
        for row in range(8):
            for col in range(8):
                zh, x, core, zl, y = move(half, row // 2, row % 2, col // 4, col % 4)
                source = (half * 8 + row) * 8 + col
                pairs.append((source, (zh * 8 + 2 * x + core) * 8 + 4 * zl + y))
    return pairs


def shift(array, move):
    return lax.ppermute(array, ALL, device_pairs(move))


def ring(array, forward, backward, beside=None):
    behind = shift(array, forward)
    ahead = shift(array, backward)
    if beside is not None:
        behind, ahead, _ = lax.optimization_barrier((behind, ahead, beside))
    far_first = shift(behind[0], forward)
    far_second = shift(ahead[1], backward)
    return array, behind, ahead, far_first, far_second


def parcels_kernel(part_ref, front_ref, out_ref):
    for c in range(8):
        out_ref[c] = front_ref[:, c * 256 : (c + 1) * 256]


def parcels(part, front):
    return pl.pallas_call(
        parcels_kernel,
        grid_spec=pltpu.PrefetchScalarGridSpec(
            num_scalar_prefetch=1,
            grid=(8,),
            in_specs=[pl.BlockSpec((128, 2048), lambda k, part: (part[0] * 8 + k, 0))],
            out_specs=pl.BlockSpec((8, 128, 256), lambda k, part: (k, 0, 0)),
        ),
        out_shape=jax.ShapeDtypeStruct((64, 128, 256), BF16),
        cost_estimate=pl.CostEstimate(flops=0, bytes_accessed=8 << 20, transcendentals=0),
        name="parcels",
    )(part.reshape(1), front)


def lower_kernel(core_ref, panel_ref, mine_ref, other_ref, out_ref):
    core = core_ref[0]
    wide = mine_ref.shape[1]
    for ref, part in ((mine_ref, core), (other_ref, 1 - core)):
        total = jnp.zeros((panel_ref.shape[1], wide), F32)
        for chunk in range(panel_ref.shape[0]):
            total += lax.dot_general(
                panel_ref[chunk],
                ref[chunk],
                (((1,), (1,)), ((), ())),
                preferred_element_type=F32,
            )
        out_ref[:, pl.ds(pl.multiple_of(part * wide, wide), wide)] = total.astype(BF16)


def lower_piece(core, panel, mine, other):
    whole = pl.BlockSpec(memory_space=pltpu.VMEM)
    return pl.pallas_call(
        lower_kernel,
        out_shape=jax.ShapeDtypeStruct((panel.shape[1], 2 * mine.shape[1]), BF16),
        in_specs=[pl.BlockSpec(memory_space=pltpu.SMEM), whole, whole, whole],
        out_specs=whole,
        compiler_params=pltpu.CompilerParams(vmem_limit_bytes=VMEM_LIMIT),
        cost_estimate=pl.CostEstimate(
            flops=2 * 256 * 1024 * 1024, bytes_accessed=3 << 20, transcendentals=0
        ),
        name="lower",
    )(core, panel, mine, other)


def update_kernel(place_ref, *refs):
    rows, mine, other = refs[0:5], refs[5:10], refs[10:15]
    out_ref, left_ref, right_ref = refs[15:18]
    child = pl.program_id(0)
    x, core, y = place_ref[0], place_ref[1], place_ref[2]

    def gather(refs, base, store):
        near, behind, ahead, far_first, far_second = refs
        store(base, near[child])
        store((base + 3) % 4, behind[child])
        store((base + 1) % 4, ahead[child])

        @pl.when(child == 0)
        def _():
            store((base + 2) % 4, far_first[...])

        @pl.when(child == 1)
        def _():
            store((base + 2) % 4, far_second[...])

    def store_rows(at, value):
        left_ref[pl.ds(pl.multiple_of(at * 256, 256), 256), :] = value

    def store_cols(which):
        def store(at, value):
            block = (at * 2 + which) * 128
            for b in range(2):
                right_ref[b, pl.ds(pl.multiple_of(block, 128), 128), :] = value[
                    b * 128 : (b + 1) * 128
                ]

        return store

    gather(rows, y, store_rows)
    gather(mine, x, store_cols(core))
    gather(other, x, store_cols(1 - core))
    for b in range(2):
        for part in range(4):
            span = slice(part * 256, (part + 1) * 256)
            out_ref[0, b, span, :] = lax.dot_general(
                left_ref[span, :],
                right_ref[b],
                (((1,), (1,)), ((), ())),
                preferred_element_type=F32,
            )


def update(place, rows, mine, other):
    whole = pl.BlockSpec(memory_space=pltpu.VMEM)
    return pl.pallas_call(
        update_kernel,
        grid=(2,),
        out_shape=jax.ShapeDtypeStruct((2, 2, 1024, 1024), F32),
        in_specs=[pl.BlockSpec(memory_space=pltpu.SMEM)] + [whole] * 15,
        out_specs=pl.BlockSpec((1, 2, 1024, 1024), lambda c: (c, 0, 0, 0)),
        scratch_shapes=[
            pltpu.VMEM((1024, 1024), BF16),
            pltpu.VMEM((2, 1024, 1024), BF16),
        ],
        compiler_params=pltpu.CompilerParams(vmem_limit_bytes=VMEM_LIMIT),
        cost_estimate=pl.CostEstimate(
            flops=2 * 4 << 30, bytes_accessed=28 << 20, transcendentals=0
        ),
        name="update",
    )(place, *rows, *mine, *other)


ROWS_STEP = 256


def place_kernel(
    flip,
    last,
    place_ref,
    front_ref,
    update_ref,
    row_map_ref,
    col_map_ref,
    base_ref,
    out_ref,
    schur_ref,
    pick_ref,
):
    b, step = pl.program_id(0), pl.program_id(1)

    @pl.when(step == 0)
    def _():
        for r in range(8):
            for c in range(8):
                rows, cols = slice(r * 128, (r + 1) * 128), slice(c * 128, (c + 1) * 128)
                entry = front_ref[r * 8 + (c ^ flip)].astype(F32)
                schur_ref[rows, cols] = (entry - update_ref[0, 0, rows, cols]).astype(BF16)
        ids = lax.broadcasted_iota(jnp.int32, (1024, 1024), 1)
        pick_ref[...] = jnp.where(col_map_ref[0] == ids, 1.0, 0.0).astype(BF16)

    first = step * ROWS_STEP
    ids = lax.broadcasted_iota(jnp.int32, (ROWS_STEP, 1024), 0) + first
    row_pick = jnp.where(row_map_ref[...] == ids, 1.0, 0.0).astype(BF16)
    rowed = jnp.dot(row_pick, schur_ref[...], preferred_element_type=F32).astype(BF16)
    placed = jnp.dot(rowed, pick_ref[...], preferred_element_type=F32)
    total = base_ref[...].astype(F32) + placed
    if last:
        shape = (ROWS_STEP, 1024)
        row_ids = lax.broadcasted_iota(jnp.int32, shape, 0) + (place_ref[3] * 1024 + first)
        col_ids = lax.broadcasted_iota(jnp.int32, shape, 1) + (
            place_ref[4] * 2048 + b * 1024
        )
        total = jnp.where(row_ids >= col_ids, total, 0.0)
    out_ref[...] = total


def place_child(place, child, front, updates, row_map, col_map, base, flip, last):
    grid_spec = pltpu.PrefetchScalarGridSpec(
        num_scalar_prefetch=1,
        grid=(2, 1024 // ROWS_STEP),
        in_specs=[
            pl.BlockSpec((64, 128, 128), lambda b, i, s: (0, 0, b)),
            pl.BlockSpec((1, 1, 1024, 1024), lambda b, i, s: (s[child], b, 0, 0)),
            pl.BlockSpec((1, 1024), lambda b, i, s: (0, 0)),
            pl.BlockSpec((1, 1024, 1), lambda b, i, s: (b, 0, 0)),
            pl.BlockSpec((ROWS_STEP, 1024), lambda b, i, s: (i, b)),
        ],
        out_specs=pl.BlockSpec((ROWS_STEP, 1024), lambda b, i, s: (i, b)),
        scratch_shapes=[
            pltpu.VMEM((1024, 1024), BF16),
            pltpu.VMEM((1024, 1024), BF16),
        ],
    )
    return pl.pallas_call(
        functools.partial(place_kernel, flip, last),
        grid_spec=grid_spec,
        out_shape=jax.ShapeDtypeStruct((1024, 2048), F32),
        compiler_params=pltpu.CompilerParams(vmem_limit_bytes=VMEM_LIMIT),
        cost_estimate=pl.CostEstimate(
            flops=2 * 4 << 30, bytes_accessed=28 << 20, transcendentals=0
        ),
        name="place_last" if last else "place_first",
    )(place, front, updates, row_map, col_map, base)


def body(front, panel, inverse_block, child_maps, root_front):
    half = lax.axis_index("half")
    row = lax.axis_index("row")
    col = lax.axis_index("col")
    x, core, zl, y = row // 2, row % 2, col // 4, col % 4
    target = half * 8 + row

    leave = parcels(1 - half, front[0])
    stay = parcels(half, front[0])
    crossed = [
        shift(
            leave[16 * part : 16 * part + 16],
            lambda zh, x, k, zl, y: (1 - zh, x, k, 1 - zl, y),
        )
        for part in range(4)
    ]

    inverse_share = lax.dynamic_slice_in_dim(inverse_block[0], core * 512, 512, 0)
    packet = jnp.concatenate(
        [panel[0].reshape(8, 256, 128), jnp.broadcast_to(inverse_share, (8, 512, 128))], 1
    )
    packet = lax.all_to_all(packet, "col", 0, 0, tiled=True)
    packet, _ = lax.optimization_barrier((packet, crossed[0]))
    own_inverse = packet[:, 256:]
    other_inverse = shift(own_inverse, lambda zh, x, k, zl, y: (zh, x, 1 - k, zl, y))
    piece = lower_piece(core.reshape(1), packet[:, :256], own_inverse, other_inverse)

    def ordered(first, second, swapped):
        return jnp.stack(
            [jnp.where(swapped, second, first), jnp.where(swapped, first, second)]
        )

    twin = shift(piece, lambda zh, x, k, zl, y: (1 - zh, x, k, zl, y))
    pair, _ = lax.optimization_barrier((ordered(piece, twin, half == 1), crossed[1]))
    columns = ring(
        pair,
        lambda zh, x, k, zl, y: (zh, (x + 1) % 4, k, zl, y),
        lambda zh, x, k, zl, y: (zh, (x + 3) % 4, k, zl, y),
        crossed[2],
    )
    columns_other = [
        shift(part, lambda zh, x, k, zl, y: (zh, x, 1 - k, zl, y)) for part in columns
    ]

    same = shift(
        lax.dynamic_slice_in_dim(piece, core * 128, 128, 0),
        lambda zh, x, k, zl, y: (zl, y, k, zh, x),
    )
    cross = shift(
        lax.dynamic_slice_in_dim(piece, (1 - core) * 128, 128, 0),
        lambda zh, x, k, zl, y: (zl, y, 1 - k, zh, x),
    )
    strip = ordered(same, cross, core == 1).reshape(256, 1024)
    strip_twin = shift(strip, lambda zh, x, k, zl, y: (zh, x, k, 1 - zl, y))
    rows = ring(
        ordered(strip, strip_twin, zl == 1),
        lambda zh, x, k, zl, y: (zh, x, k, zl, (y + 1) % 4),
        lambda zh, x, k, zl, y: (zh, x, k, zl, (y + 3) % 4),
    )

    stay, rows, columns, columns_other, _ = lax.optimization_barrier(
        (stay, rows, columns, columns_other, crossed[3])
    )
    stayed = lax.all_to_all(stay, ("row", "col"), 0, 0, tiled=True)
    crossed, stayed = lax.optimization_barrier((jnp.concatenate(crossed), stayed))
    arrived = lax.all_to_all(crossed, ("row", "col"), 0, 0, tiled=True)

    place = jnp.stack([x, core, y, target, col, half, 1 - half]).astype(jnp.int32)
    updates = update(place, rows, columns, columns_other)

    maps = child_maps.reshape(2, 8, 16, 128)
    row_maps = (
        lax.dynamic_index_in_dim(maps, target, 2, keepdims=False).reshape(2, 1, 1024)
        - target * 1024
    )
    col_maps = lax.dynamic_slice_in_dim(maps, 2 * col, 2, 2).transpose(0, 2, 1, 3)
    col_maps = col_maps - (2 * col + jnp.arange(2, dtype=jnp.int32))[None, :, None, None] * 1024
    col_maps = col_maps.reshape(2, 2, 1024, 1)

    def pick(array, which):
        return lax.dynamic_index_in_dim(array, which, 0, keepdims=False)

    summed = place_child(
        place,
        5,
        stayed,
        updates,
        pick(row_maps, half),
        pick(col_maps, half),
        root_front,
        0,
        False,
    )
    return place_child(
        place,
        6,
        arrived,
        updates,
        pick(row_maps, 1 - half),
        pick(col_maps, 1 - half),
        summed,
        4,
        True,
    )


def solution(mesh):
    return jax.shard_map(
        body,
        mesh=mesh,
        in_specs=(
            P("half", "row", "col"),
            P("half", "row", "col"),
            P("half", None, "col"),
            P(),
            P(("half", "row"), "col"),
        ),
        out_specs=P(("half", "row"), "col"),
        check_vma=False,
    )
```

```python
import jax
import jax.numpy as jnp
from jax import lax
from jax.experimental import pallas as pl
from jax.experimental.pallas import tpu as pltpu
from jax.sharding import PartitionSpec as P

ALL = ("half", "row", "col")
BF16 = jnp.bfloat16
F32 = jnp.float32
VMEM_LIMIT = 58 * 1024 * 1024
ROWS_AXIS = (((1,), (1,)), ((), ()))


def shift(array, move):
    pairs = []
    for half in range(2):
        for row in range(8):
            for col in range(8):
                h, r, c = move(half, row, col)
                pairs.append(((half * 8 + row) * 8 + col, (h * 8 + r) * 8 + c))
    return lax.ppermute(array, ALL, pairs)


LOWER_STEPS = 4
LOWER_ROWS = 512


def schur_kernel(
    place_ref,
    rows_ref,
    mine_ref,
    other_ref,
    inverse_mine_ref,
    inverse_other_ref,
    front_ref,
    out_ref,
    inverse_ref,
    wide_ref,
    left_ref,
    right_ref,
):
    step = pl.program_id(0)
    x, core = place_ref[0], place_ref[1]

    @pl.when(step == 0)
    def _():
        for ref, part in ((inverse_mine_ref, core), (inverse_other_ref, 1 - core)):
            for chunk in range(8):
                inverse_ref[
                    pl.ds(pl.multiple_of(part * 512, 512), 512),
                    chunk * 128 : (chunk + 1) * 128,
                ] = ref[chunk]

    def lower(out):
        for n in range(4):
            reach = (n + 1) * 256
            out(
                n,
                lax.dot_general(
                    wide_ref[:, :reach],
                    inverse_ref[n * 256 : reach, :reach],
                    ROWS_AXIS,
                    preferred_element_type=F32,
                ).astype(BF16),
            )

    @pl.when(step < LOWER_STEPS)
    def _():
        span = pl.ds(pl.multiple_of(step * LOWER_ROWS, LOWER_ROWS), LOWER_ROWS)

        def to_left(n, value):
            left_ref[span, n * 256 : (n + 1) * 256] = value

        def to_right(n, value):
            right_ref[span, n * 256 : (n + 1) * 256] = value

        for chunk in range(8):
            wide_ref[:, chunk * 128 : (chunk + 1) * 128] = rows_ref[chunk]
        lower(to_left)
        for ref, part in ((mine_ref, core), (other_ref, 1 - core)):
            for index, away in enumerate((0, 3, 1, 2)):
                chunk = ((x + away) % 4) * 2 + part
                wide_ref[:, pl.ds(pl.multiple_of(chunk * 128, 128), 128)] = ref[index]
        lower(to_right)

    @pl.when(step >= LOWER_STEPS)
    def _():
        at = step - LOWER_STEPS
        block = right_ref[pl.ds(pl.multiple_of(at * 256, 256), 256), :]
        for part in range(4):
            rows = slice(part * 512, (part + 1) * 512)
            product = lax.dot_general(
                left_ref[rows, :], block, ROWS_AXIS, preferred_element_type=F32
            )
            schur = (front_ref[rows, :].astype(F32) - product).astype(BF16)
            for k in range(4):
                out_ref[part * 4 + k, 0] = schur[k * 128 : (k + 1) * 128]


def schur_parcels(place, rows, mine, other, inverse_mine, inverse_other, front):
    def early(step, place):
        return jnp.minimum(step, LOWER_STEPS - 1)

    def late(step, place):
        return jnp.maximum(step - LOWER_STEPS, 0)

    grid_spec = pltpu.PrefetchScalarGridSpec(
        num_scalar_prefetch=1,
        grid=(LOWER_STEPS + 8,),
        in_specs=[
            pl.BlockSpec((8, LOWER_ROWS, 128), lambda i, s: (0, early(i, s), 0)),
            pl.BlockSpec((4, LOWER_ROWS, 128), lambda i, s: (0, early(i, s), 0)),
            pl.BlockSpec((4, LOWER_ROWS, 128), lambda i, s: (0, early(i, s), 0)),
            pl.BlockSpec((8, 512, 128), lambda i, s: (0, 0, 0)),
            pl.BlockSpec((8, 512, 128), lambda i, s: (0, 0, 0)),
            pl.BlockSpec((2048, 256), lambda i, s: (0, late(i, s))),
        ],
        out_specs=pl.BlockSpec((16, 1, 128, 256), lambda i, s: (0, late(i, s), 0, 0)),
        scratch_shapes=[
            pltpu.VMEM((1024, 1024), BF16),
            pltpu.VMEM((LOWER_ROWS, 1024), BF16),
            pltpu.VMEM((2048, 1024), BF16),
            pltpu.VMEM((2048, 1024), BF16),
        ],
    )
    return pl.pallas_call(
        schur_kernel,
        grid_spec=grid_spec,
        out_shape=jax.ShapeDtypeStruct((16, 8, 128, 256), BF16),
        compiler_params=pltpu.CompilerParams(vmem_limit_bytes=VMEM_LIMIT),
        cost_estimate=pl.CostEstimate(
            flops=14 << 30, bytes_accessed=26 << 20, transcendentals=0
        ),
        name="schur",
    )(place, rows, mine, other, inverse_mine, inverse_other, front)


def place_kernel(
    place_ref, schur_in_ref, row_map_ref, col_map_ref, base_ref, out_ref, schur_ref
):
    b, child = pl.program_id(0), pl.program_id(1)
    for r in range(8):
        for c in range(8):
            schur_ref[r * 128 : (r + 1) * 128, c * 128 : (c + 1) * 128] = schur_in_ref[
                r * 8 + c
            ]
    row_ids = lax.broadcasted_iota(jnp.int32, (1024, 1024), 0)
    col_ids = lax.broadcasted_iota(jnp.int32, (1024, 1024), 1)
    row_pick = jnp.where(row_map_ref[0] == row_ids, 1.0, 0.0).astype(BF16)
    col_pick = jnp.where(col_map_ref[0, 0] == col_ids, 1.0, 0.0).astype(BF16)
    rowed = jnp.dot(row_pick, schur_ref[...], preferred_element_type=F32).astype(BF16)
    placed = jnp.dot(rowed, col_pick, preferred_element_type=F32)

    @pl.when(child == 0)
    def _():
        out_ref[...] = base_ref[...].astype(F32) + placed

    @pl.when(child == 1)
    def _():
        rows = row_ids + place_ref[2] * 1024
        cols = col_ids + (place_ref[3] * 2048 + b * 1024)
        out_ref[...] = jnp.where(rows >= cols, out_ref[...] + placed, 0.0)


def place_children(place, arrived, row_maps, col_maps, base):
    grid_spec = pltpu.PrefetchScalarGridSpec(
        num_scalar_prefetch=1,
        grid=(2, 2),
        in_specs=[
            pl.BlockSpec((64, 128, 128), lambda b, c, s: (c, 0, b)),
            pl.BlockSpec((1, 1, 1024), lambda b, c, s: (c, 0, 0)),
            pl.BlockSpec((1, 1, 1024, 1), lambda b, c, s: (c, b, 0, 0)),
            pl.BlockSpec((1024, 1024), lambda b, c, s: (0, b)),
        ],
        out_specs=pl.BlockSpec((1024, 1024), lambda b, c, s: (0, b)),
        scratch_shapes=[pltpu.VMEM((1024, 1024), BF16)],
    )
    return pl.pallas_call(
        place_kernel,
        grid_spec=grid_spec,
        out_shape=jax.ShapeDtypeStruct((1024, 2048), F32),
        compiler_params=pltpu.CompilerParams(vmem_limit_bytes=VMEM_LIMIT),
        cost_estimate=pl.CostEstimate(
            flops=16 << 30, bytes_accessed=20 << 20, transcendentals=0
        ),
        name="place",
    )(place, arrived, row_maps, col_maps, base)


def body(front, panel, inverse_block, child_maps, root_front):
    half = lax.axis_index("half")
    row = lax.axis_index("row")
    col = lax.axis_index("col")
    x, core = row // 2, row % 2
    target = half * 8 + row
    place = jnp.stack([x, core, target, col]).astype(jnp.int32)

    rows = lax.all_gather(panel[0], "col", axis=0)
    turned = shift(panel[0], lambda h, r, c: (h, c, r))
    inverse_share = lax.dynamic_slice_in_dim(inverse_block[0], core * 512, 512, 0)
    inverse_mine = lax.all_to_all(
        jnp.broadcast_to(inverse_share, (8, 512, 128)), "col", 0, 0, tiled=True
    )
    turned, inverse_mine = lax.optimization_barrier((turned, inverse_mine))
    inverse_other = shift(inverse_mine, lambda h, r, c: (h, r ^ 1, c))
    mine = jnp.stack(
        [
            turned,
            shift(turned, lambda h, r, c: (h, (r + 2) % 8, c)),
            shift(turned, lambda h, r, c: (h, (r + 6) % 8, c)),
            shift(turned, lambda h, r, c: (h, (r + 4) % 8, c)),
        ]
    )
    other = shift(mine, lambda h, r, c: (h, r ^ 1, c))

    parcels = schur_parcels(
        place, rows, mine, other, inverse_mine, inverse_other, front[0]
    )
    arrived = lax.all_to_all(
        parcels.reshape(128, 128, 256), ALL, split_axis=0, concat_axis=0, tiled=True
    )

    maps = child_maps.reshape(2, 8, 16, 128)
    row_maps = (
        lax.dynamic_index_in_dim(maps, target, 2, keepdims=False).reshape(2, 1, 1024)
        - target * 1024
    )
    col_maps = lax.dynamic_slice_in_dim(maps, 2 * col, 2, 2).transpose(0, 2, 1, 3)
    col_maps = col_maps - (2 * col + jnp.arange(2, dtype=jnp.int32))[None, :, None, None] * 1024
    return place_children(
        place, arrived, row_maps, col_maps.reshape(2, 2, 1024, 1), root_front
    )


def solution(mesh):
    return jax.shard_map(
        body,
        mesh=mesh,
        in_specs=(
            P("half", "row", "col"),
            P("half", "row", "col"),
            P("half", None, "col"),
            P(),
            P(("half", "row"), "col"),
        ),
        out_specs=P(("half", "row"), "col"),
        check_vma=False,
    )
```

```python
import functools

import jax
import jax.numpy as jnp
from jax import lax
from jax.experimental import pallas as pl
from jax.experimental.pallas import tpu as pltpu
from jax.sharding import PartitionSpec as P

ALL = ("half", "row", "col")
BF16 = jnp.bfloat16
F32 = jnp.float32
VMEM_LIMIT = 58 * 1024 * 1024
ROWS_AXIS = (((1,), (1,)), ((), ()))


def shift(array, move):
    pairs = []
    for half in range(2):
        for row in range(8):
            for col in range(8):
                h, r, c = move(half, row, col)
                pairs.append(((half * 8 + row) * 8 + col, (h * 8 + r) * 8 + c))
    return lax.ppermute(array, ALL, pairs)


LOWER_ROWS = 512


def lower_kernel(
    place_ref,
    rows_ref,
    mine_ref,
    other_ref,
    inverse_mine_ref,
    inverse_other_ref,
    left_ref,
    right_ref,
    inverse_ref,
    wide_ref,
):
    x, core = place_ref[0], place_ref[1]

    @pl.when(pl.program_id(0) == 0)
    def _():
        for ref, part in ((inverse_mine_ref, core), (inverse_other_ref, 1 - core)):
            for chunk in range(8):
                inverse_ref[
                    pl.ds(pl.multiple_of(part * 512, 512), 512),
                    chunk * 128 : (chunk + 1) * 128,
                ] = ref[chunk]

    def lower(out_ref):
        for n in range(4):
            reach = (n + 1) * 256
            out_ref[:, n * 256 : reach] = lax.dot_general(
                wide_ref[:, :reach],
                inverse_ref[n * 256 : reach, :reach],
                ROWS_AXIS,
                preferred_element_type=F32,
            ).astype(BF16)

    for chunk in range(8):
        wide_ref[:, chunk * 128 : (chunk + 1) * 128] = rows_ref[chunk]
    lower(left_ref)
    for ref, part in ((mine_ref, core), (other_ref, 1 - core)):
        for index, away in enumerate((0, 3, 1, 2)):
            chunk = ((x + away) % 4) * 2 + part
            wide_ref[:, pl.ds(pl.multiple_of(chunk * 128, 128), 128)] = ref[index]
    lower(right_ref)


def lower_rows(place, packet, mine, other, inverse_other):
    out = jax.ShapeDtypeStruct((2048, 1024), BF16)
    grid_spec = pltpu.PrefetchScalarGridSpec(
        num_scalar_prefetch=1,
        grid=(2048 // LOWER_ROWS,),
        in_specs=[
            pl.BlockSpec((8, LOWER_ROWS, 128), lambda i, s: (0, i, 0)),
            pl.BlockSpec((4, LOWER_ROWS, 128), lambda i, s: (0, i, 0)),
            pl.BlockSpec((4, LOWER_ROWS, 128), lambda i, s: (0, i, 0)),
            pl.BlockSpec((8, 512, 128), lambda i, s: (0, 4, 0)),
            pl.BlockSpec((8, 512, 128), lambda i, s: (0, 0, 0)),
        ],
        out_specs=[pl.BlockSpec((LOWER_ROWS, 1024), lambda i, s: (i, 0))] * 2,
        scratch_shapes=[
            pltpu.VMEM((1024, 1024), BF16),
            pltpu.VMEM((LOWER_ROWS, 1024), BF16),
        ],
    )
    return pl.pallas_call(
        lower_kernel,
        grid_spec=grid_spec,
        out_shape=[out, out],
        compiler_params=pltpu.CompilerParams(vmem_limit_bytes=VMEM_LIMIT),
        cost_estimate=pl.CostEstimate(
            flops=5 << 30, bytes_accessed=18 << 20, transcendentals=0
        ),
        name="lower",
    )(place, packet, mine, other, packet, inverse_other)


def schur_kernel(left_ref, right_ref, front_even_ref, front_odd_ref, out_ref):
    block = right_ref[...].reshape(256, 1024)
    for part in range(4):
        rows = slice(part * 512, (part + 1) * 512)
        product = lax.dot_general(
            left_ref[rows, :], block, ROWS_AXIS, preferred_element_type=F32
        )
        for which, front_ref in enumerate((front_even_ref, front_odd_ref)):
            lanes = slice(which * 128, (which + 1) * 128)
            schur = (front_ref[rows, :].astype(F32) - product[:, lanes]).astype(BF16)
            for k in range(4):
                out_ref[part * 4 + k, which] = schur[k * 128 : (k + 1) * 128]


def schur_parcels(b, left, right, front):
    return pl.pallas_call(
        schur_kernel,
        grid=(4,),
        in_specs=[
            pl.BlockSpec((2048, 1024), lambda i: (0, 0)),
            pl.BlockSpec((2, 1, 128, 1024), lambda i: (i, b, 0, 0)),
            pl.BlockSpec((2048, 128), lambda i: (0, 4 * i + b)),
            pl.BlockSpec((2048, 128), lambda i: (0, 4 * i + 2 + b)),
        ],
        out_specs=pl.BlockSpec((16, 2, 128, 128), lambda i: (0, i, 0, 0)),
        out_shape=jax.ShapeDtypeStruct((16, 8, 128, 128), BF16),
        compiler_params=pltpu.CompilerParams(vmem_limit_bytes=VMEM_LIMIT),
        cost_estimate=pl.CostEstimate(
            flops=4 << 30, bytes_accessed=14 << 20, transcendentals=0
        ),
        name="schur",
    )(left, right.reshape(8, 2, 128, 1024), front, front)


def place_kernel(
    b, place_ref, schur_in_ref, row_map_ref, col_map_ref, base_ref, *refs
):
    out_ref, schur_ref = refs[-2:]
    child = pl.program_id(0)
    for r in range(8):
        for c in range(8):
            schur_ref[r * 128 : (r + 1) * 128, c * 128 : (c + 1) * 128] = schur_in_ref[
                r * 8 + c
            ]
    row_ids = lax.broadcasted_iota(jnp.int32, (1024, 1024), 0)
    col_ids = lax.broadcasted_iota(jnp.int32, (1024, 1024), 1)
    row_pick = jnp.where(row_map_ref[0] == row_ids, 1.0, 0.0).astype(BF16)
    col_pick = jnp.where(col_map_ref[0, 0] == col_ids, 1.0, 0.0).astype(BF16)
    rowed = jnp.dot(row_pick, schur_ref[...], preferred_element_type=F32).astype(BF16)
    placed = jnp.dot(rowed, col_pick, preferred_element_type=F32)

    @pl.when(child == 0)
    def _():
        out_ref[...] = base_ref[...].astype(F32) + placed

    @pl.when(child == 1)
    def _():
        rows = row_ids + place_ref[2] * 1024
        cols = col_ids + (place_ref[3] * 2048 + b * 1024)
        out_ref[...] = jnp.where(rows >= cols, out_ref[...] + placed, 0.0)


def place_children(b, place, arrived, row_maps, col_maps, base, half_done=None):
    grid_spec = pltpu.PrefetchScalarGridSpec(
        num_scalar_prefetch=1,
        grid=(2,),
        in_specs=[
            pl.BlockSpec((64, 128, 128), lambda c, s: (c, 0, 0)),
            pl.BlockSpec((1, 1, 1024), lambda c, s: (c, 0, 0)),
            pl.BlockSpec((1, 1, 1024, 1), lambda c, s: (c, b, 0, 0)),
            pl.BlockSpec((1024, 1024), lambda c, s: (0, b)),
        ]
        + ([] if half_done is None else [pl.BlockSpec(memory_space=pl.ANY)]),
        out_specs=pl.BlockSpec((1024, 1024), lambda c, s: (0, b)),
        scratch_shapes=[pltpu.VMEM((1024, 1024), BF16)],
    )
    return pl.pallas_call(
        functools.partial(place_kernel, b),
        grid_spec=grid_spec,
        out_shape=jax.ShapeDtypeStruct((1024, 2048), F32),
        input_output_aliases={} if half_done is None else {5: 0},
        compiler_params=pltpu.CompilerParams(vmem_limit_bytes=VMEM_LIMIT),
        cost_estimate=pl.CostEstimate(
            flops=8 << 30, bytes_accessed=10 << 20, transcendentals=0
        ),
        name="place",
    )(
        place,
        arrived,
        row_maps,
        col_maps,
        base,
        *(() if half_done is None else (half_done,)),
    )


def body(front, panel, inverse_block, child_maps, root_front):
    half = lax.axis_index("half")
    row = lax.axis_index("row")
    col = lax.axis_index("col")
    x, core = row // 2, row % 2
    target = half * 8 + row
    place = jnp.stack([x, core, target, col]).astype(jnp.int32)

    turned = shift(panel[0], lambda h, r, c: (h, c, r))
    inverse_share = lax.dynamic_slice_in_dim(inverse_block[0], core * 512, 512, 0)
    packet = jnp.concatenate([panel[0], inverse_share])
    packet = lax.all_to_all(
        jnp.broadcast_to(packet, (8, 2560, 128)), "col", 0, 0, tiled=True
    )
    inverse_other = shift(packet[:, 2048:], lambda h, r, c: (h, r ^ 1, c))
    mine = jnp.stack(
        [
            turned,
            shift(turned, lambda h, r, c: (h, (r + 2) % 8, c)),
            shift(turned, lambda h, r, c: (h, (r + 6) % 8, c)),
            shift(turned, lambda h, r, c: (h, (r + 4) % 8, c)),
        ]
    )
    other = shift(mine, lambda h, r, c: (h, r ^ 1, c))
    left, right = lower_rows(place, packet, mine, other, inverse_other)

    maps = child_maps.reshape(2, 8, 16, 128)
    row_maps = (
        lax.dynamic_index_in_dim(maps, target, 2, keepdims=False).reshape(2, 1, 1024)
        - target * 1024
    )
    col_maps = lax.dynamic_slice_in_dim(maps, 2 * col, 2, 2).transpose(0, 2, 1, 3)
    col_maps = col_maps - (2 * col + jnp.arange(2, dtype=jnp.int32))[None, :, None, None] * 1024
    col_maps = col_maps.reshape(2, 2, 1024, 1)

    out = None
    for b in range(2):
        parcels = schur_parcels(b, left, right, front[0])
        arrived = lax.all_to_all(parcels.reshape(128, 128, 128), ALL, 0, 0, tiled=True)
        out = place_children(b, place, arrived, row_maps, col_maps, root_front, out)
    return out


def solution(mesh):
    return jax.shard_map(
        body,
        mesh=mesh,
        in_specs=(
            P("half", "row", "col"),
            P("half", "row", "col"),
            P("half", None, "col"),
            P(),
            P(("half", "row"), "col"),
        ),
        out_specs=P(("half", "row"), "col"),
        check_vma=False,
    )
```

```python
import functools

import jax
import jax.numpy as jnp
from jax import lax
from jax.experimental import pallas as pl
from jax.experimental.pallas import tpu as pltpu
from jax.sharding import PartitionSpec as P

ALL = ("half", "row", "col")
BF16 = jnp.bfloat16
F32 = jnp.float32
VMEM_LIMIT = 58 * 1024 * 1024
ROWS_AXIS = (((1,), (1,)), ((), ()))


def shift(array, move):
    pairs = []
    for half in range(2):
        for row in range(8):
            for col in range(8):
                h, r, c = move(half, row, col)
                pairs.append(((half * 8 + row) * 8 + col, (h * 8 + r) * 8 + c))
    return lax.ppermute(array, ALL, pairs)


LOWER_ROWS = 512


def lower_kernel(
    place_ref,
    near_ref,
    behind_ref,
    ahead_ref,
    far_first_ref,
    far_second_ref,
    mine_ref,
    other_ref,
    inverse_mine_ref,
    inverse_other_ref,
    left_ref,
    right_ref,
    inverse_ref,
    wide_ref,
):
    x, core, y = place_ref[0], place_ref[1], place_ref[4]

    def columns(chunk):
        return pl.ds(pl.multiple_of(chunk * 128, 128), 128)

    @pl.when(pl.program_id(0) == 0)
    def _():
        for ref, part in ((inverse_mine_ref, core), (inverse_other_ref, 1 - core)):
            for index, away in enumerate((0, 3, 1, 2)):
                inverse_ref[:, columns(((x + away) % 4) * 2 + part)] = ref[index]

    def lower(out_ref):
        for n in range(4):
            reach = (n + 1) * 256
            out_ref[:, n * 256 : reach] = lax.dot_general(
                wide_ref[:, :reach],
                inverse_ref[n * 256 : reach, :reach],
                ROWS_AXIS,
                preferred_element_type=F32,
            ).astype(BF16)

    for ref, away in ((near_ref, 0), (behind_ref, 3), (ahead_ref, 1)):
        for zl in range(2):
            wide_ref[:, columns(zl * 4 + (y + away) % 4)] = ref[zl]
    wide_ref[:, columns((y + 2) % 4)] = far_first_ref[...]
    wide_ref[:, columns(4 + (y + 2) % 4)] = far_second_ref[...]
    lower(left_ref)
    for ref, part in ((mine_ref, core), (other_ref, 1 - core)):
        for index, away in enumerate((0, 3, 1, 2)):
            wide_ref[:, columns(((x + away) % 4) * 2 + part)] = ref[index]
    lower(right_ref)


def lower_rows(place, rows, mine, other):
    out = jax.ShapeDtypeStruct((2048, 1024), BF16)
    pair = pl.BlockSpec((2, LOWER_ROWS, 128), lambda i, s: (0, i, 0))
    single = pl.BlockSpec((LOWER_ROWS, 128), lambda i, s: (i, 0))
    four = pl.BlockSpec((4, LOWER_ROWS, 128), lambda i, s: (0, i, 0))
    inverse = pl.BlockSpec((4, 1024, 128), lambda i, s: (0, 2, 0))
    grid_spec = pltpu.PrefetchScalarGridSpec(
        num_scalar_prefetch=1,
        grid=(2048 // LOWER_ROWS,),
        in_specs=[pair] * 3 + [single] * 2 + [four] * 2 + [inverse] * 2,
        out_specs=[pl.BlockSpec((LOWER_ROWS, 1024), lambda i, s: (i, 0))] * 2,
        scratch_shapes=[
            pltpu.VMEM((1024, 1024), BF16),
            pltpu.VMEM((LOWER_ROWS, 1024), BF16),
        ],
    )
    return pl.pallas_call(
        lower_kernel,
        grid_spec=grid_spec,
        out_shape=[out, out],
        compiler_params=pltpu.CompilerParams(vmem_limit_bytes=VMEM_LIMIT),
        cost_estimate=pl.CostEstimate(
            flops=5 << 30, bytes_accessed=18 << 20, transcendentals=0
        ),
        name="lower",
    )(place, *rows, mine, other, mine, other)


def schur_kernel(left_ref, right_ref, front_even_ref, front_odd_ref, out_ref):
    block = right_ref[...].reshape(256, 1024)
    for part in range(4):
        rows = slice(part * 512, (part + 1) * 512)
        product = lax.dot_general(
            left_ref[rows, :], block, ROWS_AXIS, preferred_element_type=F32
        )
        for which, front_ref in enumerate((front_even_ref, front_odd_ref)):
            lanes = slice(which * 128, (which + 1) * 128)
            schur = (front_ref[rows, :].astype(F32) - product[:, lanes]).astype(BF16)
            for k in range(4):
                out_ref[part * 4 + k, which] = schur[k * 128 : (k + 1) * 128]


def schur_parcels(b, left, right, front):
    return pl.pallas_call(
        schur_kernel,
        grid=(4,),
        in_specs=[
            pl.BlockSpec((2048, 1024), lambda i: (0, 0)),
            pl.BlockSpec((2, 1, 128, 1024), lambda i: (i, b, 0, 0)),
            pl.BlockSpec((2048, 128), lambda i: (0, 4 * i + b)),
            pl.BlockSpec((2048, 128), lambda i: (0, 4 * i + 2 + b)),
        ],
        out_specs=pl.BlockSpec((16, 2, 128, 128), lambda i: (0, i, 0, 0)),
        out_shape=jax.ShapeDtypeStruct((16, 8, 128, 128), BF16),
        compiler_params=pltpu.CompilerParams(vmem_limit_bytes=VMEM_LIMIT),
        cost_estimate=pl.CostEstimate(
            flops=4 << 30, bytes_accessed=14 << 20, transcendentals=0
        ),
        name="schur",
    )(left, right.reshape(8, 2, 128, 1024), front, front)


def place_kernel(
    b, place_ref, schur_in_ref, row_map_ref, col_map_ref, base_ref, *refs
):
    out_ref, schur_ref = refs[-2:]
    child = pl.program_id(0)
    for r in range(8):
        for c in range(8):
            schur_ref[r * 128 : (r + 1) * 128, c * 128 : (c + 1) * 128] = schur_in_ref[
                r * 8 + c
            ]
    row_ids = lax.broadcasted_iota(jnp.int32, (1024, 1024), 0)
    col_ids = lax.broadcasted_iota(jnp.int32, (1024, 1024), 1)
    row_pick = jnp.where(row_map_ref[0] == row_ids, 1.0, 0.0).astype(BF16)
    col_pick = jnp.where(col_map_ref[0, 0] == col_ids, 1.0, 0.0).astype(BF16)
    rowed = jnp.dot(row_pick, schur_ref[...], preferred_element_type=F32).astype(BF16)
    placed = jnp.dot(rowed, col_pick, preferred_element_type=F32)

    @pl.when(child == 0)
    def _():
        out_ref[...] = base_ref[...].astype(F32) + placed

    @pl.when(child == 1)
    def _():
        rows = row_ids + place_ref[2] * 1024
        cols = col_ids + (place_ref[3] * 2048 + b * 1024)
        out_ref[...] = jnp.where(rows >= cols, out_ref[...] + placed, 0.0)


def place_children(b, place, arrived, row_maps, col_maps, base, half_done=None):
    grid_spec = pltpu.PrefetchScalarGridSpec(
        num_scalar_prefetch=1,
        grid=(2,),
        in_specs=[
            pl.BlockSpec((64, 128, 128), lambda c, s: (c, 0, 0)),
            pl.BlockSpec((1, 1, 1024), lambda c, s: (c, 0, 0)),
            pl.BlockSpec((1, 1, 1024, 1), lambda c, s: (c, b, 0, 0)),
            pl.BlockSpec((1024, 1024), lambda c, s: (0, b)),
        ]
        + ([] if half_done is None else [pl.BlockSpec(memory_space=pl.ANY)]),
        out_specs=pl.BlockSpec((1024, 1024), lambda c, s: (0, b)),
        scratch_shapes=[pltpu.VMEM((1024, 1024), BF16)],
    )
    return pl.pallas_call(
        functools.partial(place_kernel, b),
        grid_spec=grid_spec,
        out_shape=jax.ShapeDtypeStruct((1024, 2048), F32),
        input_output_aliases={} if half_done is None else {5: 0},
        compiler_params=pltpu.CompilerParams(vmem_limit_bytes=VMEM_LIMIT),
        cost_estimate=pl.CostEstimate(
            flops=8 << 30, bytes_accessed=10 << 20, transcendentals=0
        ),
        name="place",
    )(
        place,
        arrived,
        row_maps,
        col_maps,
        base,
        *(() if half_done is None else (half_done,)),
    )


def body(front, panel, inverse_block, child_maps, root_front):
    half = lax.axis_index("half")
    row = lax.axis_index("row")
    col = lax.axis_index("col")
    x, core = row // 2, row % 2
    target = half * 8 + row
    place = jnp.stack([x, core, target, col, col % 4]).astype(jnp.int32)

    turned = shift(
        jnp.concatenate([panel[0], inverse_block[0]]), lambda h, r, c: (h, c, r)
    )
    twin = shift(panel[0], lambda h, r, c: (h, r, c ^ 4))
    pair = jnp.stack(
        [jnp.where(col < 4, panel[0], twin), jnp.where(col < 4, twin, panel[0])]
    )

    def forward(h, r, c):
        return h, r, c // 4 * 4 + (c + 1) % 4

    def backward(h, r, c):
        return h, r, c // 4 * 4 + (c + 3) % 4

    turned, pair = lax.optimization_barrier((turned, pair))
    one = shift(turned, lambda h, r, c: (h, (r + 2) % 8, c))
    three = shift(turned, lambda h, r, c: (h, (r + 6) % 8, c))
    behind = shift(pair, forward)
    ahead = shift(pair, backward)
    two = shift(turned, lambda h, r, c: (h, (r + 4) % 8, c))
    one, three, behind, ahead = lax.optimization_barrier((one, three, behind, ahead))
    far_first, far_second, two = lax.optimization_barrier(
        (shift(behind[0], forward), shift(ahead[1], backward), two)
    )
    rows = (pair, behind, ahead, far_first, far_second)
    mine = jnp.stack([turned, one, three, two])
    other = shift(mine, lambda h, r, c: (h, r ^ 1, c))
    left, right = lower_rows(place, rows, mine, other)

    maps = child_maps.reshape(2, 8, 16, 128)
    row_maps = (
        lax.dynamic_index_in_dim(maps, target, 2, keepdims=False).reshape(2, 1, 1024)
        - target * 1024
    )
    col_maps = lax.dynamic_slice_in_dim(maps, 2 * col, 2, 2).transpose(0, 2, 1, 3)
    col_maps = col_maps - (2 * col + jnp.arange(2, dtype=jnp.int32))[None, :, None, None] * 1024
    col_maps = col_maps.reshape(2, 2, 1024, 1)

    out = None
    for b in range(2):
        parcels = schur_parcels(b, left, right, front[0])
        arrived = lax.all_to_all(parcels.reshape(128, 128, 128), ALL, 0, 0, tiled=True)
        out = place_children(b, place, arrived, row_maps, col_maps, root_front, out)
    return out


def solution(mesh):
    return jax.shard_map(
        body,
        mesh=mesh,
        in_specs=(
            P("half", "row", "col"),
            P("half", "row", "col"),
            P("half", None, "col"),
            P(),
            P(("half", "row"), "col"),
        ),
        out_specs=P(("half", "row"), "col"),
        check_vma=False,
    )
```

```python
import functools

import jax
import jax.numpy as jnp
from jax import lax
from jax.experimental import pallas as pl
from jax.experimental.pallas import tpu as pltpu
from jax.sharding import PartitionSpec as P

ALL = ("half", "row", "col")
BF16 = jnp.bfloat16
F32 = jnp.float32
VMEM_LIMIT = 58 * 1024 * 1024
ROWS_AXIS = (((1,), (1,)), ((), ()))


def shift(array, move):
    pairs = []
    for half in range(2):
        for row in range(8):
            for col in range(8):
                h, r, c = move(half, row, col)
                pairs.append(((half * 8 + row) * 8 + col, (h * 8 + r) * 8 + c))
    return lax.ppermute(array, ALL, pairs)


LOWER_ROWS = 1024


def lower_kernel(
    place_ref,
    near_ref,
    behind_ref,
    ahead_ref,
    far_first_ref,
    far_second_ref,
    mine_ref,
    other_ref,
    inverse_mine_ref,
    inverse_other_ref,
    left_ref,
    right_ref,
    inverse_ref,
    wide_ref,
):
    turn, core, y = place_ref[0], place_ref[1], place_ref[4]

    def columns(chunk):
        return pl.ds(pl.multiple_of(chunk * 128, 128), 128)

    @pl.when(pl.program_id(0) == 0)
    def _():
        for ref, part in ((inverse_mine_ref, core), (inverse_other_ref, 1 - core)):
            for index, away in enumerate((0, 3, 1, 2)):
                inverse_ref[:, columns(((turn + away) % 4) * 2 + part)] = ref[index]

    def lower(out_ref):
        for n in range(4):
            reach = (n + 1) * 256
            out_ref[:, n * 256 : reach] = lax.dot_general(
                wide_ref[:, :reach],
                inverse_ref[n * 256 : reach, :reach],
                ROWS_AXIS,
                preferred_element_type=F32,
            ).astype(BF16)

    for ref, away in ((near_ref, 0), (behind_ref, 3), (ahead_ref, 1)):
        for zl in range(2):
            wide_ref[:, columns(zl * 4 + (y + away) % 4)] = ref[zl]
    wide_ref[:, columns((y + 2) % 4)] = far_first_ref[...]
    wide_ref[:, columns(4 + (y + 2) % 4)] = far_second_ref[...]
    lower(left_ref)
    for ref, part in ((mine_ref, core), (other_ref, 1 - core)):
        for index, away in enumerate((0, 3, 1, 2)):
            wide_ref[:, columns(((turn + away) % 4) * 2 + part)] = ref[index]
    lower(right_ref)


def lower_rows(place, rows, mine, other):
    out = jax.ShapeDtypeStruct((2048, 1024), BF16)
    pair = pl.BlockSpec((2, LOWER_ROWS, 128), lambda i, s: (0, i, 0))
    single = pl.BlockSpec((LOWER_ROWS, 128), lambda i, s: (i, 0))
    four = pl.BlockSpec((4, LOWER_ROWS, 128), lambda i, s: (0, i, 0))
    inverse = pl.BlockSpec((4, 1024, 128), lambda i, s: (0, 2, 0))
    grid_spec = pltpu.PrefetchScalarGridSpec(
        num_scalar_prefetch=1,
        grid=(2048 // LOWER_ROWS,),
        in_specs=[pair] * 3 + [single] * 2 + [four] * 2 + [inverse] * 2,
        out_specs=[pl.BlockSpec((LOWER_ROWS, 1024), lambda i, s: (i, 0))] * 2,
        scratch_shapes=[
            pltpu.VMEM((1024, 1024), BF16),
            pltpu.VMEM((LOWER_ROWS, 1024), BF16),
        ],
    )
    return pl.pallas_call(
        lower_kernel,
        grid_spec=grid_spec,
        out_shape=[out, out],
        compiler_params=pltpu.CompilerParams(vmem_limit_bytes=VMEM_LIMIT),
        cost_estimate=pl.CostEstimate(
            flops=5 << 30, bytes_accessed=18 << 20, transcendentals=0
        ),
        name="lower",
    )(place, *rows, mine, other, mine, other)


def schur_kernel(left_ref, right_ref, front_even_ref, front_odd_ref, out_ref):
    block = right_ref[...].reshape(256, 1024)
    product = lax.dot_general(
        left_ref[...], block, ROWS_AXIS, preferred_element_type=F32
    )
    for which, front_ref in enumerate((front_even_ref, front_odd_ref)):
        lanes = slice(which * 128, (which + 1) * 128)
        for k in range(16):
            rows = slice(k * 128, (k + 1) * 128)
            out_ref[k, which] = (
                front_ref[rows, :].astype(F32) - product[rows, lanes]
            ).astype(BF16)


def schur_parcels(b, left, right, front):
    return pl.pallas_call(
        schur_kernel,
        grid=(4,),
        in_specs=[
            pl.BlockSpec((2048, 1024), lambda i: (0, 0)),
            pl.BlockSpec((2, 1, 128, 1024), lambda i: (i, b, 0, 0)),
            pl.BlockSpec((2048, 128), lambda i: (0, 4 * i + b)),
            pl.BlockSpec((2048, 128), lambda i: (0, 4 * i + 2 + b)),
        ],
        out_specs=pl.BlockSpec((16, 2, 128, 128), lambda i: (0, i, 0, 0)),
        out_shape=jax.ShapeDtypeStruct((16, 8, 128, 128), BF16),
        compiler_params=pltpu.CompilerParams(vmem_limit_bytes=VMEM_LIMIT),
        cost_estimate=pl.CostEstimate(
            flops=4 << 30, bytes_accessed=14 << 20, transcendentals=0
        ),
        name="schur",
    )(left, right.reshape(8, 2, 128, 1024), front, front)


def place_kernel(
    b, place_ref, schur_in_ref, row_map_ref, col_map_ref, base_ref, *refs
):
    out_ref, schur_ref = refs[-2:]
    child = pl.program_id(0)
    for r in range(8):
        for c in range(8):
            schur_ref[r * 128 : (r + 1) * 128, c * 128 : (c + 1) * 128] = schur_in_ref[
                r * 8 + c
            ]
    row_ids = lax.broadcasted_iota(jnp.int32, (1024, 1024), 0)
    col_ids = lax.broadcasted_iota(jnp.int32, (1024, 1024), 1)
    row_pick = jnp.where(row_map_ref[0] == row_ids, 1.0, 0.0).astype(BF16)
    col_pick = jnp.where(col_map_ref[0, 0] == col_ids, 1.0, 0.0).astype(BF16)
    rowed = jnp.dot(row_pick, schur_ref[...], preferred_element_type=F32).astype(BF16)
    placed = jnp.dot(rowed, col_pick, preferred_element_type=F32)

    @pl.when(child == 0)
    def _():
        out_ref[...] = base_ref[...].astype(F32) + placed

    @pl.when(child == 1)
    def _():
        rows = row_ids + place_ref[2] * 1024
        cols = col_ids + (place_ref[3] * 2048 + b * 1024)
        out_ref[...] = jnp.where(rows >= cols, out_ref[...] + placed, 0.0)


def place_children(b, place, arrived, row_maps, col_maps, base, half_done=None):
    grid_spec = pltpu.PrefetchScalarGridSpec(
        num_scalar_prefetch=1,
        grid=(2,),
        in_specs=[
            pl.BlockSpec((64, 128, 128), lambda c, s: (c, 0, 0)),
            pl.BlockSpec((1, 1, 1024), lambda c, s: (c, 0, 0)),
            pl.BlockSpec((1, 1, 1024, 1), lambda c, s: (c, b, 0, 0)),
            pl.BlockSpec((1024, 1024), lambda c, s: (0, b)),
        ]
        + ([] if half_done is None else [pl.BlockSpec(memory_space=pl.ANY)]),
        out_specs=pl.BlockSpec((1024, 1024), lambda c, s: (0, b)),
        scratch_shapes=[pltpu.VMEM((1024, 1024), BF16)],
    )
    return pl.pallas_call(
        functools.partial(place_kernel, b),
        grid_spec=grid_spec,
        out_shape=jax.ShapeDtypeStruct((1024, 2048), F32),
        input_output_aliases={} if half_done is None else {5: 0},
        compiler_params=pltpu.CompilerParams(vmem_limit_bytes=VMEM_LIMIT),
        cost_estimate=pl.CostEstimate(
            flops=8 << 30, bytes_accessed=10 << 20, transcendentals=0
        ),
        name="place",
    )(
        place,
        arrived,
        row_maps,
        col_maps,
        base,
        *(() if half_done is None else (half_done,)),
    )


def body(front, panel, inverse_block, child_maps, root_front):
    half = lax.axis_index("half")
    row = lax.axis_index("row")
    col = lax.axis_index("col")
    x, core = row // 2, row % 2
    target = half * 8 + row
    place = jnp.stack([(x + 4 - col // 2) % 4, core, target, col, col % 4]).astype(jnp.int32)

    turned = shift(
        jnp.concatenate([panel[0], inverse_block[0]]), lambda h, r, c: (h, (c // 2 + r // 2) % 4 * 2 + c % 2, r)
    )
    twin = shift(panel[0], lambda h, r, c: (h, r, c ^ 4))
    pair = jnp.stack(
        [jnp.where(col < 4, panel[0], twin), jnp.where(col < 4, twin, panel[0])]
    )

    def forward(h, r, c):
        return h, r, c // 4 * 4 + (c + 1) % 4

    def backward(h, r, c):
        return h, r, c // 4 * 4 + (c + 3) % 4

    turned, pair = lax.optimization_barrier((turned, pair))
    one = shift(turned, lambda h, r, c: (h, (r + 2) % 8, c))
    three = shift(turned, lambda h, r, c: (h, (r + 6) % 8, c))
    behind = shift(pair, forward)
    ahead = shift(pair, backward)
    two = shift(turned, lambda h, r, c: (h, (r + 4) % 8, c))
    one, three, behind, ahead = lax.optimization_barrier((one, three, behind, ahead))
    far_first, far_second, two = lax.optimization_barrier(
        (shift(behind[0], forward), shift(ahead[1], backward), two)
    )
    rows = (pair, behind, ahead, far_first, far_second)
    mine = jnp.stack([turned, one, three, two])
    other = shift(mine, lambda h, r, c: (h, r ^ 1, c))
    left, right = lower_rows(place, rows, mine, other)

    maps = child_maps.reshape(2, 8, 16, 128)
    row_maps = (
        lax.dynamic_index_in_dim(maps, target, 2, keepdims=False).reshape(2, 1, 1024)
        - target * 1024
    )
    col_maps = lax.dynamic_slice_in_dim(maps, 2 * col, 2, 2).transpose(0, 2, 1, 3)
    col_maps = col_maps - (2 * col + jnp.arange(2, dtype=jnp.int32))[None, :, None, None] * 1024
    col_maps = col_maps.reshape(2, 2, 1024, 1)

    out = None
    for b in range(2):
        parcels = schur_parcels(b, left, right, front[0])
        arrived = lax.all_to_all(parcels.reshape(128, 128, 128), ALL, 0, 0, tiled=True)
        out = place_children(b, place, arrived, row_maps, col_maps, root_front, out)
    return out


def solution(mesh):
    return jax.shard_map(
        body,
        mesh=mesh,
        in_specs=(
            P("half", "row", "col"),
            P("half", "row", "col"),
            P("half", None, "col"),
            P(),
            P(("half", "row"), "col"),
        ),
        out_specs=P(("half", "row"), "col"),
        check_vma=False,
    )
```

```python
import functools

import jax
import jax.numpy as jnp
from jax import lax
from jax.experimental import pallas as pl
from jax.experimental.pallas import tpu as pltpu
from jax.sharding import PartitionSpec as P

ALL = ("half", "row", "col")
BF16 = jnp.bfloat16
F32 = jnp.float32
VMEM_LIMIT = 58 * 1024 * 1024
ROWS_AXIS = (((1,), (1,)), ((), ()))


def shift(array, move):
    pairs = []
    for half in range(2):
        for row in range(8):
            for col in range(8):
                h, r, c = move(half, row, col)
                pairs.append(((half * 8 + row) * 8 + col, (h * 8 + r) * 8 + c))
    return lax.ppermute(array, ALL, pairs)


def spans(chunk):
    return pl.ds(pl.multiple_of(chunk * 128, 128), 128)


def gather_columns(place_ref, mine_ref, other_ref, out_ref):
    turn, core = place_ref[0], place_ref[1]
    for ref, part in ((mine_ref, core), (other_ref, 1 - core)):
        for index, away in enumerate((0, 3, 1, 2)):
            out_ref[:, spans((turn + away) % 4 * 2 + part)] = ref[index]


def inverse_product(wide_ref, inverse_ref, out_ref):
    for n in range(4):
        reach = (n + 1) * 256
        out_ref[:, n * 256 : reach] = lax.dot_general(
            wide_ref[:, :reach],
            inverse_ref[n * 256 : reach, :reach],
            ROWS_AXIS,
            preferred_element_type=F32,
        ).astype(BF16)


def first_kernel(
    place_ref,
    near_ref,
    behind_ref,
    ahead_ref,
    far_first_ref,
    far_second_ref,
    mine_ref,
    other_ref,
    inverse_mine_ref,
    inverse_other_ref,
    right_ref,
    left_ref,
    inverse_ref,
    wide_ref,
):
    y = place_ref[4]

    @pl.when(pl.program_id(0) == 0)
    def _():
        gather_columns(place_ref, inverse_mine_ref, inverse_other_ref, inverse_ref)
        gather_columns(place_ref, mine_ref, other_ref, wide_ref)
        inverse_product(wide_ref, inverse_ref, right_ref)

    @pl.when(pl.program_id(0) > 0)
    def _():
        for ref, away in ((near_ref, 0), (behind_ref, 3), (ahead_ref, 1)):
            for zl in range(2):
                wide_ref[:, spans(zl * 4 + (y + away) % 4)] = ref[zl]
        wide_ref[:, spans((y + 2) % 4)] = far_first_ref[...]
        wide_ref[:, spans(4 + (y + 2) % 4)] = far_second_ref[...]
        inverse_product(wide_ref, inverse_ref, left_ref)


FOUR_PANELS = pl.BlockSpec((4, 1024, 128), lambda i, s: (0, 0, 0))
FOUR_INVERSES = pl.BlockSpec((4, 1024, 128), lambda i, s: (0, 1, 0))
SQUARE = (1024, 1024)


def lower_first(place, rows, mine, other):
    def part(i):
        return jnp.maximum(i - 1, 0)

    pair = pl.BlockSpec((2, 1024, 128), lambda i, s: (0, part(i), 0))
    single = pl.BlockSpec((1024, 128), lambda i, s: (part(i), 0))
    grid_spec = pltpu.PrefetchScalarGridSpec(
        num_scalar_prefetch=1,
        grid=(3,),
        in_specs=[pair] * 3 + [single] * 2 + [FOUR_PANELS] * 2 + [FOUR_INVERSES] * 2,
        out_specs=[
            pl.BlockSpec(SQUARE, lambda i, s: (0, 0)),
            pl.BlockSpec(SQUARE, lambda i, s: (part(i), 0)),
        ],
        scratch_shapes=[pltpu.VMEM(SQUARE, BF16), pltpu.VMEM(SQUARE, BF16)],
    )
    return pl.pallas_call(
        first_kernel,
        grid_spec=grid_spec,
        out_shape=[
            jax.ShapeDtypeStruct(SQUARE, BF16),
            jax.ShapeDtypeStruct((2048, 1024), BF16),
        ],
        compiler_params=pltpu.CompilerParams(vmem_limit_bytes=VMEM_LIMIT),
        cost_estimate=pl.CostEstimate(
            flops=4 << 30, bytes_accessed=14 << 20, transcendentals=0
        ),
        name="lower_first",
    )(place, *rows, mine, other, mine, other)


def right_kernel(
    place_ref,
    mine_ref,
    other_ref,
    inverse_mine_ref,
    inverse_other_ref,
    out_ref,
    inverse_ref,
    wide_ref,
):
    gather_columns(place_ref, inverse_mine_ref, inverse_other_ref, inverse_ref)
    gather_columns(place_ref, mine_ref, other_ref, wide_ref)
    inverse_product(wide_ref, inverse_ref, out_ref)


def lower_right(place, mine, other, inverse_mine, inverse_other):
    grid_spec = pltpu.PrefetchScalarGridSpec(
        num_scalar_prefetch=1,
        grid=(1,),
        in_specs=[FOUR_PANELS] * 2 + [FOUR_INVERSES] * 2,
        out_specs=pl.BlockSpec(SQUARE, lambda i, s: (0, 0)),
        scratch_shapes=[pltpu.VMEM(SQUARE, BF16), pltpu.VMEM(SQUARE, BF16)],
    )
    return pl.pallas_call(
        right_kernel,
        grid_spec=grid_spec,
        out_shape=jax.ShapeDtypeStruct(SQUARE, BF16),
        compiler_params=pltpu.CompilerParams(vmem_limit_bytes=VMEM_LIMIT),
        cost_estimate=pl.CostEstimate(
            flops=3 << 29, bytes_accessed=6 << 20, transcendentals=0
        ),
        name="lower_right",
    )(place, mine, other, inverse_mine, inverse_other)


def schur_kernel(left_ref, right_ref, front_even_ref, front_odd_ref, out_ref):
    product = lax.dot_general(
        left_ref[...], right_ref[...], ROWS_AXIS, preferred_element_type=F32
    )
    for which, front_ref in enumerate((front_even_ref, front_odd_ref)):
        lanes = slice(which * 128, (which + 1) * 128)
        for k in range(16):
            rows = slice(k * 128, (k + 1) * 128)
            out_ref[k, which] = (
                front_ref[rows, :].astype(F32) - product[rows, lanes]
            ).astype(BF16)


def schur_parcels(b, left, right, front):
    return pl.pallas_call(
        schur_kernel,
        grid=(4,),
        in_specs=[
            pl.BlockSpec((2048, 1024), lambda i: (0, 0)),
            pl.BlockSpec((256, 1024), lambda i: (i, 0)),
            pl.BlockSpec((2048, 128), lambda i: (0, 4 * i + b)),
            pl.BlockSpec((2048, 128), lambda i: (0, 4 * i + 2 + b)),
        ],
        out_specs=pl.BlockSpec((16, 2, 128, 128), lambda i: (0, i, 0, 0)),
        out_shape=jax.ShapeDtypeStruct((16, 8, 128, 128), BF16),
        compiler_params=pltpu.CompilerParams(vmem_limit_bytes=VMEM_LIMIT),
        cost_estimate=pl.CostEstimate(
            flops=4 << 30, bytes_accessed=14 << 20, transcendentals=0
        ),
        name="schur",
    )(left, right, front, front)


def place_kernel(
    b, place_ref, schur_in_ref, row_map_ref, col_map_ref, base_ref, *refs
):
    out_ref, schur_ref = refs[-2:]
    child = pl.program_id(0)
    for r in range(8):
        for c in range(8):
            schur_ref[r * 128 : (r + 1) * 128, c * 128 : (c + 1) * 128] = schur_in_ref[
                r * 8 + c
            ]
    row_ids = lax.broadcasted_iota(jnp.int32, (1024, 1024), 0)
    col_ids = lax.broadcasted_iota(jnp.int32, (1024, 1024), 1)
    row_pick = jnp.where(row_map_ref[0] == row_ids, 1.0, 0.0).astype(BF16)
    col_pick = jnp.where(col_map_ref[0, 0] == col_ids, 1.0, 0.0).astype(BF16)
    rowed = jnp.dot(row_pick, schur_ref[...], preferred_element_type=F32).astype(BF16)
    placed = jnp.dot(rowed, col_pick, preferred_element_type=F32)

    @pl.when(child == 0)
    def _():
        out_ref[...] = base_ref[...].astype(F32) + placed

    @pl.when(child == 1)
    def _():
        rows = row_ids + place_ref[2] * 1024
        cols = col_ids + (place_ref[3] * 2048 + b * 1024)
        out_ref[...] = jnp.where(rows >= cols, out_ref[...] + placed, 0.0)


def place_children(b, place, arrived, row_maps, col_maps, base, half_done=None):
    grid_spec = pltpu.PrefetchScalarGridSpec(
        num_scalar_prefetch=1,
        grid=(2,),
        in_specs=[
            pl.BlockSpec((64, 128, 128), lambda c, s: (c, 0, 0)),
            pl.BlockSpec((1, 1, 1024), lambda c, s: (c, 0, 0)),
            pl.BlockSpec((1, 1, 1024, 1), lambda c, s: (c, b, 0, 0)),
            pl.BlockSpec((1024, 1024), lambda c, s: (0, b)),
        ]
        + ([] if half_done is None else [pl.BlockSpec(memory_space=pl.ANY)]),
        out_specs=pl.BlockSpec((1024, 1024), lambda c, s: (0, b)),
        scratch_shapes=[pltpu.VMEM((1024, 1024), BF16)],
    )
    return pl.pallas_call(
        functools.partial(place_kernel, b),
        grid_spec=grid_spec,
        out_shape=jax.ShapeDtypeStruct((1024, 2048), F32),
        input_output_aliases={} if half_done is None else {5: 0},
        compiler_params=pltpu.CompilerParams(vmem_limit_bytes=VMEM_LIMIT),
        cost_estimate=pl.CostEstimate(
            flops=8 << 30, bytes_accessed=10 << 20, transcendentals=0
        ),
        name="place",
    )(
        place,
        arrived,
        row_maps,
        col_maps,
        base,
        *(() if half_done is None else (half_done,)),
    )


def body(front, panel, inverse_block, child_maps, root_front):
    half = lax.axis_index("half")
    row = lax.axis_index("row")
    col = lax.axis_index("col")
    x, core = row // 2, row % 2
    target = half * 8 + row
    place = jnp.stack([(x + 4 - col // 2) % 4, core, target, col, col % 4]).astype(jnp.int32)

    def spread(array):
        return shift(array, lambda h, r, c: (h, (c // 2 + r // 2) % 4 * 2 + c % 2, r))

    def ahead_x(array):
        return shift(array, lambda h, r, c: (h, (r + 2) % 8, c))

    def behind_x(array):
        return shift(array, lambda h, r, c: (h, (r + 6) % 8, c))

    def ahead_y(array):
        return shift(array, lambda h, r, c: (h, r, c // 4 * 4 + (c + 1) % 4))

    def behind_y(array):
        return shift(array, lambda h, r, c: (h, r, c // 4 * 4 + (c + 3) % 4))

    def swap_core(array):
        return shift(array, lambda h, r, c: (h, r ^ 1, c))

    runs = panel[0].reshape(8, 2, 128, 128)
    even = spread(jnp.concatenate([runs[:, 0].reshape(1024, 128), inverse_block[0]]))
    odd = spread(runs[:, 1].reshape(1024, 128))
    twin = shift(panel[0], lambda h, r, c: (h, r, c ^ 4))
    pair = jnp.stack(
        [jnp.where(col < 4, panel[0], twin), jnp.where(col < 4, twin, panel[0])]
    )
    even, pair = lax.optimization_barrier((even, pair))
    one, three, behind, ahead, odd = lax.optimization_barrier(
        (ahead_x(even), behind_x(even), ahead_y(pair), behind_y(pair), odd)
    )
    far_first, far_second, two_first, two_second, odd_one, odd_three = (
        lax.optimization_barrier(
            (
                ahead_y(behind[0]),
                behind_y(ahead[1]),
                ahead_x(one[:1024]),
                behind_x(three[1024:]),
                ahead_x(odd),
                behind_x(odd),
            )
        )
    )
    rows = (pair, behind, ahead, far_first, far_second)
    mine = jnp.stack([even, one, three, jnp.concatenate([two_first, two_second])])
    other, odd_two_first, odd_two_second = lax.optimization_barrier(
        (swap_core(mine), ahead_x(odd_one[:512]), behind_x(odd_three[512:]))
    )
    right_even, left = lower_first(place, rows, mine, other)
    odd_two = jnp.concatenate([odd_two_first, odd_two_second])
    odd_mine = jnp.stack([odd, odd_one, odd_three, odd_two])
    odd_other = swap_core(odd_mine)

    maps = child_maps.reshape(2, 8, 16, 128)
    row_maps = (
        lax.dynamic_index_in_dim(maps, target, 2, keepdims=False).reshape(2, 1, 1024)
        - target * 1024
    )
    col_maps = lax.dynamic_slice_in_dim(maps, 2 * col, 2, 2).transpose(0, 2, 1, 3)
    col_maps = col_maps - (2 * col + jnp.arange(2, dtype=jnp.int32))[None, :, None, None] * 1024
    col_maps = col_maps.reshape(2, 2, 1024, 1)

    def exchange(parcels):
        return lax.all_to_all(parcels.reshape(128, 128, 128), ALL, 0, 0, tiled=True)

    def placed(b, arrived, done=None):
        return place_children(b, place, arrived, row_maps, col_maps, root_front, done)

    parcels = schur_parcels(0, left, right_even, front[0])
    parcels, odd_mine, odd_other = lax.optimization_barrier((parcels, odd_mine, odd_other))
    arrived = exchange(parcels)
    right_odd = lower_right(place, odd_mine, odd_other, mine, other)
    arrived_odd = exchange(schur_parcels(1, left, right_odd, front[0]))
    return placed(1, arrived_odd, placed(0, arrived))


def solution(mesh):
    return jax.shard_map(
        body,
        mesh=mesh,
        in_specs=(
            P("half", "row", "col"),
            P("half", "row", "col"),
            P("half", None, "col"),
            P(),
            P(("half", "row"), "col"),
        ),
        out_specs=P(("half", "row"), "col"),
        check_vma=False,
    )
```

```python
import functools

import jax
import jax.numpy as jnp
from jax import lax
from jax.experimental import pallas as pl
from jax.experimental.pallas import tpu as pltpu
from jax.sharding import PartitionSpec as P

ALL = ("half", "row", "col")
BF16 = jnp.bfloat16
F32 = jnp.float32
VMEM_LIMIT = 58 * 1024 * 1024
ROWS_AXIS = (((1,), (1,)), ((), ()))


def shift(array, move):
    pairs = []
    for half in range(2):
        for row in range(8):
            for col in range(8):
                h, r, c = move(half, row, col)
                pairs.append(((half * 8 + row) * 8 + col, (h * 8 + r) * 8 + c))
    return lax.ppermute(array, ALL, pairs)


def spans(chunk):
    return pl.ds(pl.multiple_of(chunk * 128, 128), 128)


def gather_columns(place_ref, mine_ref, other_ref, out_ref):
    turn, core = place_ref[0], place_ref[1]
    for ref, part in ((mine_ref, core), (other_ref, 1 - core)):
        for index, away in enumerate((0, 3, 1, 2)):
            out_ref[:, spans((turn + away) % 4 * 2 + part)] = ref[index]


def inverse_product(wide_ref, inverse_ref, out_ref):
    for n in range(4):
        reach = (n + 1) * 256
        out_ref[:, n * 256 : reach] = lax.dot_general(
            wide_ref[:, :reach],
            inverse_ref[n * 256 : reach, :reach],
            ROWS_AXIS,
            preferred_element_type=F32,
        ).astype(BF16)


def first_kernel(
    place_ref,
    near_ref,
    behind_ref,
    ahead_ref,
    far_first_ref,
    far_second_ref,
    below_mine_ref,
    below_other_ref,
    mine_ref,
    other_ref,
    inverse_mine_ref,
    inverse_other_ref,
    right_ref,
    left_ref,
    inverse_ref,
    wide_ref,
):
    step = pl.program_id(0)
    y, z = place_ref[4], place_ref[3] // 4

    @pl.when(step == 0)
    def _():
        gather_columns(place_ref, inverse_mine_ref, inverse_other_ref, inverse_ref)
        gather_columns(place_ref, mine_ref, other_ref, wide_ref)
        inverse_product(wide_ref, inverse_ref, right_ref)

    @pl.when(step == 1)
    def _():
        for ref, away in ((near_ref, 0), (behind_ref, 3), (ahead_ref, 1)):
            for side in range(2):
                wide_ref[:, spans(side * 4 + (y + away) % 4)] = ref[side]
        wide_ref[:, spans((y + 2) % 4)] = far_first_ref[...]
        wide_ref[:, spans(4 + (y + 2) % 4)] = far_second_ref[...]
        inverse_product(wide_ref, inverse_ref, left_ref)

    @pl.when(step == 2)
    def _():
        for ref, side in ((below_mine_ref, z), (below_other_ref, 1 - z)):
            for index, away in enumerate((0, 3, 1, 2)):
                wide_ref[:, spans(side * 4 + (y + away) % 4)] = ref[index]
        inverse_product(wide_ref, inverse_ref, left_ref)


FOUR_PANELS = pl.BlockSpec((4, 1024, 128), lambda i, s: (0, 0, 0))
FOUR_INVERSES = pl.BlockSpec((4, 1024, 128), lambda i, s: (0, 1, 0))
SQUARE = (1024, 1024)


def lower_first(place, rows, mine, other):
    def part(i):
        return jnp.maximum(i - 1, 0)

    pair = pl.BlockSpec((2, 1024, 128), lambda i, s: (0, 0, 0))
    single = pl.BlockSpec((1024, 128), lambda i, s: (0, 0))
    grid_spec = pltpu.PrefetchScalarGridSpec(
        num_scalar_prefetch=1,
        grid=(3,),
        in_specs=[pair] * 3 + [single] * 2 + [FOUR_PANELS] * 4 + [FOUR_INVERSES] * 2,
        out_specs=[
            pl.BlockSpec(SQUARE, lambda i, s: (0, 0)),
            pl.BlockSpec(SQUARE, lambda i, s: (part(i), 0)),
        ],
        scratch_shapes=[pltpu.VMEM(SQUARE, BF16), pltpu.VMEM(SQUARE, BF16)],
    )
    return pl.pallas_call(
        first_kernel,
        grid_spec=grid_spec,
        out_shape=[
            jax.ShapeDtypeStruct(SQUARE, BF16),
            jax.ShapeDtypeStruct((2048, 1024), BF16),
        ],
        compiler_params=pltpu.CompilerParams(vmem_limit_bytes=VMEM_LIMIT),
        cost_estimate=pl.CostEstimate(
            flops=4 << 30, bytes_accessed=14 << 20, transcendentals=0
        ),
        name="lower_first",
    )(place, *rows, mine, other, mine, other)


def right_kernel(
    place_ref,
    mine_ref,
    other_ref,
    inverse_mine_ref,
    inverse_other_ref,
    out_ref,
    inverse_ref,
    wide_ref,
):
    gather_columns(place_ref, inverse_mine_ref, inverse_other_ref, inverse_ref)
    gather_columns(place_ref, mine_ref, other_ref, wide_ref)
    inverse_product(wide_ref, inverse_ref, out_ref)


def lower_right(place, mine, other, inverse_mine, inverse_other):
    grid_spec = pltpu.PrefetchScalarGridSpec(
        num_scalar_prefetch=1,
        grid=(1,),
        in_specs=[FOUR_PANELS] * 2 + [FOUR_INVERSES] * 2,
        out_specs=pl.BlockSpec(SQUARE, lambda i, s: (0, 0)),
        scratch_shapes=[pltpu.VMEM(SQUARE, BF16), pltpu.VMEM(SQUARE, BF16)],
    )
    return pl.pallas_call(
        right_kernel,
        grid_spec=grid_spec,
        out_shape=jax.ShapeDtypeStruct(SQUARE, BF16),
        compiler_params=pltpu.CompilerParams(vmem_limit_bytes=VMEM_LIMIT),
        cost_estimate=pl.CostEstimate(
            flops=3 << 29, bytes_accessed=6 << 20, transcendentals=0
        ),
        name="lower_right",
    )(place, mine, other, inverse_mine, inverse_other)


def schur_kernel(left_ref, right_ref, front_even_ref, front_odd_ref, out_ref):
    product = lax.dot_general(
        left_ref[...], right_ref[...], ROWS_AXIS, preferred_element_type=F32
    )
    for which, front_ref in enumerate((front_even_ref, front_odd_ref)):
        lanes = slice(which * 128, (which + 1) * 128)
        for k in range(16):
            rows = slice(k * 128, (k + 1) * 128)
            out_ref[k, which] = (
                front_ref[rows, :].astype(F32) - product[rows, lanes]
            ).astype(BF16)


def schur_parcels(b, left, right, front):
    return pl.pallas_call(
        schur_kernel,
        grid=(4,),
        in_specs=[
            pl.BlockSpec((2048, 1024), lambda i: (0, 0)),
            pl.BlockSpec((256, 1024), lambda i: (i, 0)),
            pl.BlockSpec((2048, 128), lambda i: (0, 4 * i + b)),
            pl.BlockSpec((2048, 128), lambda i: (0, 4 * i + 2 + b)),
        ],
        out_specs=pl.BlockSpec((16, 2, 128, 128), lambda i: (0, i, 0, 0)),
        out_shape=jax.ShapeDtypeStruct((16, 8, 128, 128), BF16),
        compiler_params=pltpu.CompilerParams(vmem_limit_bytes=VMEM_LIMIT),
        cost_estimate=pl.CostEstimate(
            flops=4 << 30, bytes_accessed=14 << 20, transcendentals=0
        ),
        name="schur",
    )(left, right, front, front)


def place_kernel(
    b, place_ref, schur_in_ref, row_map_ref, col_map_ref, base_ref, *refs
):
    out_ref, schur_ref = refs[-2:]
    child = pl.program_id(0)
    for r in range(8):
        for c in range(8):
            schur_ref[r * 128 : (r + 1) * 128, c * 128 : (c + 1) * 128] = schur_in_ref[
                r * 8 + c
            ]
    row_ids = lax.broadcasted_iota(jnp.int32, (1024, 1024), 0)
    col_ids = lax.broadcasted_iota(jnp.int32, (1024, 1024), 1)
    row_pick = jnp.where(row_map_ref[0] == row_ids, 1.0, 0.0).astype(BF16)
    col_pick = jnp.where(col_map_ref[0, 0] == col_ids, 1.0, 0.0).astype(BF16)
    rowed = jnp.dot(row_pick, schur_ref[...], preferred_element_type=F32).astype(BF16)
    placed = jnp.dot(rowed, col_pick, preferred_element_type=F32)

    @pl.when(child == 0)
    def _():
        out_ref[...] = base_ref[...].astype(F32) + placed

    @pl.when(child == 1)
    def _():
        rows = row_ids + place_ref[2] * 1024
        cols = col_ids + (place_ref[3] * 2048 + b * 1024)
        out_ref[...] = jnp.where(rows >= cols, out_ref[...] + placed, 0.0)


def place_children(b, place, arrived, row_maps, col_maps, base, half_done=None):
    grid_spec = pltpu.PrefetchScalarGridSpec(
        num_scalar_prefetch=1,
        grid=(2,),
        in_specs=[
            pl.BlockSpec((64, 128, 128), lambda c, s: (c, 0, 0)),
            pl.BlockSpec((1, 1, 1024), lambda c, s: (c, 0, 0)),
            pl.BlockSpec((1, 1, 1024, 1), lambda c, s: (c, b, 0, 0)),
            pl.BlockSpec((1024, 1024), lambda c, s: (0, b)),
        ]
        + ([] if half_done is None else [pl.BlockSpec(memory_space=pl.ANY)]),
        out_specs=pl.BlockSpec((1024, 1024), lambda c, s: (0, b)),
        scratch_shapes=[pltpu.VMEM((1024, 1024), BF16)],
    )
    return pl.pallas_call(
        functools.partial(place_kernel, b),
        grid_spec=grid_spec,
        out_shape=jax.ShapeDtypeStruct((1024, 2048), F32),
        input_output_aliases={} if half_done is None else {5: 0},
        compiler_params=pltpu.CompilerParams(vmem_limit_bytes=VMEM_LIMIT),
        cost_estimate=pl.CostEstimate(
            flops=8 << 30, bytes_accessed=10 << 20, transcendentals=0
        ),
        name="place",
    )(
        place,
        arrived,
        row_maps,
        col_maps,
        base,
        *(() if half_done is None else (half_done,)),
    )


def body(front, panel, inverse_block, child_maps, root_front):
    half = lax.axis_index("half")
    row = lax.axis_index("row")
    col = lax.axis_index("col")
    x, core = row // 2, row % 2
    target = half * 8 + row
    place = jnp.stack([(x + 4 - col // 2) % 4, core, target, col, col % 4]).astype(jnp.int32)

    def spread(array):
        return shift(array, lambda h, r, c: (h, (c // 2 + r // 2) % 4 * 2 + c % 2, r))

    def ahead_x(array):
        return shift(array, lambda h, r, c: (h, (r + 2) % 8, c))

    def behind_x(array):
        return shift(array, lambda h, r, c: (h, (r + 6) % 8, c))

    def ahead_y(array):
        return shift(array, lambda h, r, c: (h, r, c // 4 * 4 + (c + 1) % 4))

    def behind_y(array):
        return shift(array, lambda h, r, c: (h, r, c // 4 * 4 + (c + 3) % 4))

    def swap_z(array):
        return shift(array, lambda h, r, c: (h, r, c ^ 4))

    def swap_core(array):
        return shift(array, lambda h, r, c: (h, r ^ 1, c))

    runs = panel[0].reshape(8, 2, 128, 128)
    even = spread(jnp.concatenate([runs[:, 0].reshape(1024, 128), inverse_block[0]]))
    odd = spread(runs[:, 1].reshape(1024, 128))
    upper, below = panel[0, :1024], panel[0, 1024:]
    even, twin, below_one, below_three, below_two = lax.optimization_barrier(
        (
            even,
            swap_z(upper),
            ahead_y(below),
            behind_y(below),
            shift(below, lambda h, r, c: (h, r, c ^ 2)),
        )
    )
    pair = jnp.stack([jnp.where(col < 4, upper, twin), jnp.where(col < 4, twin, upper)])
    below_mine = jnp.stack([below, below_one, below_three, below_two])
    one, three, behind, ahead = lax.optimization_barrier(
        (ahead_x(even), behind_x(even), ahead_y(pair), behind_y(pair))
    )
    below_other = swap_z(below_mine)
    far_first, far_second, two_first, two_second, odd, below_other = lax.optimization_barrier(
        (
            ahead_y(behind[0]),
            behind_y(ahead[1]),
            ahead_x(one[:1024]),
            behind_x(three[1024:]),
            odd,
            below_other,
        )
    )
    mine = jnp.stack([even, one, three, jnp.concatenate([two_first, two_second])])
    other = swap_core(mine)
    rows = (pair, behind, ahead, far_first, far_second, below_mine, below_other)
    odd_parts = (
        ahead_x(odd),
        behind_x(odd),
        shift(odd, lambda h, r, c: (h, r ^ 4, c)),
    )
    right_even, left = lower_first(place, rows, mine, other)
    odd_parts, right_even, left = lax.optimization_barrier((odd_parts, right_even, left))
    odd_mine = jnp.stack([odd, *odd_parts])
    odd_other = swap_core(odd_mine)

    maps = child_maps.reshape(2, 8, 16, 128)
    row_maps = (
        lax.dynamic_index_in_dim(maps, target, 2, keepdims=False).reshape(2, 1, 1024)
        - target * 1024
    )
    col_maps = lax.dynamic_slice_in_dim(maps, 2 * col, 2, 2).transpose(0, 2, 1, 3)
    col_maps = col_maps - (2 * col + jnp.arange(2, dtype=jnp.int32))[None, :, None, None] * 1024
    col_maps = col_maps.reshape(2, 2, 1024, 1)

    def exchange(parcels):
        return lax.all_to_all(parcels.reshape(128, 128, 128), ALL, 0, 0, tiled=True)

    def placed(b, arrived, done=None):
        return place_children(b, place, arrived, row_maps, col_maps, root_front, done)

    parcels = schur_parcels(0, left, right_even, front[0])
    parcels, odd_mine, odd_other = lax.optimization_barrier((parcels, odd_mine, odd_other))
    arrived = exchange(parcels)
    right_odd = lower_right(place, odd_mine, odd_other, mine, other)
    arrived_odd = exchange(schur_parcels(1, left, right_odd, front[0]))
    return placed(1, arrived_odd, placed(0, arrived))


def solution(mesh):
    return jax.shard_map(
        body,
        mesh=mesh,
        in_specs=(
            P("half", "row", "col"),
            P("half", "row", "col"),
            P("half", None, "col"),
            P(),
            P(("half", "row"), "col"),
        ),
        out_specs=P(("half", "row"), "col"),
        check_vma=False,
    )
```

```python
import functools

import jax
import jax.numpy as jnp
from jax import lax
from jax.experimental import pallas as pl
from jax.experimental.pallas import tpu as pltpu
from jax.sharding import PartitionSpec as P

ALL = ("half", "row", "col")
BF16 = jnp.bfloat16
F32 = jnp.float32
VMEM_LIMIT = 58 * 1024 * 1024
ROWS_AXIS = (((1,), (1,)), ((), ()))


def shift(array, move):
    pairs = []
    for half in range(2):
        for row in range(8):
            for col in range(8):
                h, r, c = move(half, row, col)
                pairs.append(((half * 8 + row) * 8 + col, (h * 8 + r) * 8 + c))
    return lax.ppermute(array, ALL, pairs)


def spans(chunk):
    return pl.ds(pl.multiple_of(chunk * 128, 128), 128)


def gather_columns(place_ref, mine_ref, other_ref, out_ref):
    turn, core = place_ref[0], place_ref[1]
    for ref, part in ((mine_ref, core), (other_ref, 1 - core)):
        for index, away in enumerate((0, 3, 1, 2)):
            out_ref[:, spans((turn + away) % 4 * 2 + part)] = ref[index]


def inverse_product(wide_ref, inverse_ref, out_ref):
    for n in range(4):
        reach = (n + 1) * 256
        out_ref[:, n * 256 : reach] = lax.dot_general(
            wide_ref[:, :reach],
            inverse_ref[n * 256 : reach, :reach],
            ROWS_AXIS,
            preferred_element_type=F32,
        ).astype(BF16)


def first_kernel(
    place_ref,
    near_ref,
    behind_ref,
    ahead_ref,
    far_first_ref,
    far_second_ref,
    below_mine_ref,
    below_other_ref,
    mine_ref,
    other_ref,
    inverse_mine_ref,
    inverse_other_ref,
    right_ref,
    left_ref,
    inverse_ref,
    wide_ref,
):
    step = pl.program_id(0)
    y, z = place_ref[4], place_ref[3] // 4

    @pl.when(step == 0)
    def _():
        gather_columns(place_ref, inverse_mine_ref, inverse_other_ref, inverse_ref)
        gather_columns(place_ref, mine_ref, other_ref, wide_ref)
        inverse_product(wide_ref, inverse_ref, right_ref)

    @pl.when(step == 1)
    def _():
        for ref, away in ((near_ref, 0), (behind_ref, 3), (ahead_ref, 1)):
            for side in range(2):
                wide_ref[:, spans(side * 4 + (y + away) % 4)] = ref[side]
        wide_ref[:, spans((y + 2) % 4)] = far_first_ref[...]
        wide_ref[:, spans(4 + (y + 2) % 4)] = far_second_ref[...]
        inverse_product(wide_ref, inverse_ref, left_ref)

    @pl.when(step == 2)
    def _():
        for ref, side in ((below_mine_ref, z), (below_other_ref, 1 - z)):
            for index, away in enumerate((0, 3, 1, 2)):
                wide_ref[:, spans(side * 4 + (y + away) % 4)] = ref[index]
        inverse_product(wide_ref, inverse_ref, left_ref)


FOUR_PANELS = pl.BlockSpec((4, 1024, 128), lambda i, s: (0, 0, 0))
FOUR_INVERSES = pl.BlockSpec((4, 1024, 128), lambda i, s: (0, 1, 0))
SQUARE = (1024, 1024)


def lower_first(place, rows, mine, other):
    def part(i):
        return jnp.maximum(i - 1, 0)

    pair = pl.BlockSpec((2, 1024, 128), lambda i, s: (0, 0, 0))
    single = pl.BlockSpec((1024, 128), lambda i, s: (0, 0))
    grid_spec = pltpu.PrefetchScalarGridSpec(
        num_scalar_prefetch=1,
        grid=(3,),
        in_specs=[pair] * 3 + [single] * 2 + [FOUR_PANELS] * 4 + [FOUR_INVERSES] * 2,
        out_specs=[
            pl.BlockSpec(SQUARE, lambda i, s: (0, 0)),
            pl.BlockSpec(SQUARE, lambda i, s: (part(i), 0)),
        ],
        scratch_shapes=[pltpu.VMEM(SQUARE, BF16), pltpu.VMEM(SQUARE, BF16)],
    )
    return pl.pallas_call(
        first_kernel,
        grid_spec=grid_spec,
        out_shape=[
            jax.ShapeDtypeStruct(SQUARE, BF16),
            jax.ShapeDtypeStruct((2048, 1024), BF16),
        ],
        compiler_params=pltpu.CompilerParams(vmem_limit_bytes=VMEM_LIMIT),
        cost_estimate=pl.CostEstimate(
            flops=4 << 30, bytes_accessed=14 << 20, transcendentals=0
        ),
        name="lower_first",
    )(place, *rows, mine, other, mine, other)


def right_kernel(
    place_ref,
    mine_ref,
    other_ref,
    inverse_mine_ref,
    inverse_other_ref,
    out_ref,
    inverse_ref,
    wide_ref,
):
    gather_columns(place_ref, inverse_mine_ref, inverse_other_ref, inverse_ref)
    gather_columns(place_ref, mine_ref, other_ref, wide_ref)
    inverse_product(wide_ref, inverse_ref, out_ref)


def lower_right(place, mine, other, inverse_mine, inverse_other):
    grid_spec = pltpu.PrefetchScalarGridSpec(
        num_scalar_prefetch=1,
        grid=(1,),
        in_specs=[FOUR_PANELS] * 2 + [FOUR_INVERSES] * 2,
        out_specs=pl.BlockSpec(SQUARE, lambda i, s: (0, 0)),
        scratch_shapes=[pltpu.VMEM(SQUARE, BF16), pltpu.VMEM(SQUARE, BF16)],
    )
    return pl.pallas_call(
        right_kernel,
        grid_spec=grid_spec,
        out_shape=jax.ShapeDtypeStruct(SQUARE, BF16),
        compiler_params=pltpu.CompilerParams(vmem_limit_bytes=VMEM_LIMIT),
        cost_estimate=pl.CostEstimate(
            flops=3 << 29, bytes_accessed=6 << 20, transcendentals=0
        ),
        name="lower_right",
    )(place, mine, other, inverse_mine, inverse_other)


def schur_kernel(left_ref, right_ref, front_even_ref, front_odd_ref, out_ref):
    product = lax.dot_general(
        left_ref[...], right_ref[...], ROWS_AXIS, preferred_element_type=F32
    )
    for which, front_ref in enumerate((front_even_ref, front_odd_ref)):
        lanes = slice(which * 128, (which + 1) * 128)
        for k in range(16):
            rows = slice(k * 128, (k + 1) * 128)
            out_ref[k, which] = (
                front_ref[rows, :].astype(F32) - product[rows, lanes]
            ).astype(BF16)


def schur_parcels(b, left, right, front):
    return pl.pallas_call(
        schur_kernel,
        grid=(4,),
        in_specs=[
            pl.BlockSpec((2048, 1024), lambda i: (0, 0)),
            pl.BlockSpec((256, 1024), lambda i: (i, 0)),
            pl.BlockSpec((2048, 128), lambda i: (0, 4 * i + b)),
            pl.BlockSpec((2048, 128), lambda i: (0, 4 * i + 2 + b)),
        ],
        out_specs=pl.BlockSpec((16, 2, 128, 128), lambda i: (0, i, 0, 0)),
        out_shape=jax.ShapeDtypeStruct((16, 8, 128, 128), BF16),
        compiler_params=pltpu.CompilerParams(vmem_limit_bytes=VMEM_LIMIT),
        cost_estimate=pl.CostEstimate(
            flops=4 << 30, bytes_accessed=14 << 20, transcendentals=0
        ),
        name="schur",
    )(left, right, front, front)


def place_kernel(
    b, place_ref, schur_in_ref, row_map_ref, col_map_ref, base_ref, *refs
):
    out_ref, schur_ref = refs[-2:]
    child = pl.program_id(0)
    for r in range(8):
        for c in range(8):
            schur_ref[r * 128 : (r + 1) * 128, c * 128 : (c + 1) * 128] = schur_in_ref[
                r * 8 + c
            ]
    row_ids = lax.broadcasted_iota(jnp.int32, (1024, 1024), 0)
    col_ids = lax.broadcasted_iota(jnp.int32, (1024, 1024), 1)
    row_pick = jnp.where(row_map_ref[0] == row_ids, 1.0, 0.0).astype(BF16)
    col_pick = jnp.where(col_map_ref[0, 0] == col_ids, 1.0, 0.0).astype(BF16)
    rowed = jnp.dot(row_pick, schur_ref[...], preferred_element_type=F32).astype(BF16)
    placed = jnp.dot(rowed, col_pick, preferred_element_type=F32)

    @pl.when(child == 0)
    def _():
        out_ref[...] = base_ref[...].astype(F32) + placed

    @pl.when(child == 1)
    def _():
        rows = row_ids + place_ref[2] * 1024
        cols = col_ids + (place_ref[3] * 2048 + b * 1024)
        out_ref[...] = jnp.where(rows >= cols, out_ref[...] + placed, 0.0)


def place_children(b, place, arrived, row_maps, col_maps, base, half_done=None):
    grid_spec = pltpu.PrefetchScalarGridSpec(
        num_scalar_prefetch=1,
        grid=(2,),
        in_specs=[
            pl.BlockSpec((64, 128, 128), lambda c, s: (c, 0, 0)),
            pl.BlockSpec((1, 1, 1024), lambda c, s: (c, 0, 0)),
            pl.BlockSpec((1, 1, 1024, 1), lambda c, s: (c, b, 0, 0)),
            pl.BlockSpec((1024, 1024), lambda c, s: (0, b)),
        ]
        + ([] if half_done is None else [pl.BlockSpec(memory_space=pl.ANY)]),
        out_specs=pl.BlockSpec((1024, 1024), lambda c, s: (0, b)),
        scratch_shapes=[pltpu.VMEM((1024, 1024), BF16)],
    )
    return pl.pallas_call(
        functools.partial(place_kernel, b),
        grid_spec=grid_spec,
        out_shape=jax.ShapeDtypeStruct((1024, 2048), F32),
        input_output_aliases={} if half_done is None else {5: 0},
        compiler_params=pltpu.CompilerParams(vmem_limit_bytes=VMEM_LIMIT),
        cost_estimate=pl.CostEstimate(
            flops=8 << 30, bytes_accessed=10 << 20, transcendentals=0
        ),
        name="place",
    )(
        place,
        arrived,
        row_maps,
        col_maps,
        base,
        *(() if half_done is None else (half_done,)),
    )


def body(front, panel, inverse_block, child_maps, root_front):
    half = lax.axis_index("half")
    row = lax.axis_index("row")
    col = lax.axis_index("col")
    x, core = row // 2, row % 2
    target = half * 8 + row
    place = jnp.stack([(x + 4 - col // 2) % 4, core, target, col, col % 4]).astype(jnp.int32)

    def spread(array):
        return shift(array, lambda h, r, c: (h, (c // 2 + r // 2) % 4 * 2 + c % 2, r))

    def ahead_x(array):
        return shift(array, lambda h, r, c: (h, (r + 2) % 8, c))

    def behind_x(array):
        return shift(array, lambda h, r, c: (h, (r + 6) % 8, c))

    def ahead_y(array):
        return shift(array, lambda h, r, c: (h, r, c // 4 * 4 + (c + 1) % 4))

    def behind_y(array):
        return shift(array, lambda h, r, c: (h, r, c // 4 * 4 + (c + 3) % 4))

    def swap_z(array):
        return shift(array, lambda h, r, c: (h, r, c ^ 4))

    def swap_core(array):
        return shift(array, lambda h, r, c: (h, r ^ 1, c))

    runs = panel[0].reshape(8, 2, 128, 128)
    turned = spread(
        jnp.concatenate(
            [
                runs[:, 0].reshape(1024, 128),
                inverse_block[0],
                runs[:, 1].reshape(1024, 128),
            ]
        )
    )
    upper, below = panel[0, :1024], panel[0, 1024:]
    turned, twin, below_one, below_three, below_two = lax.optimization_barrier(
        (
            turned,
            swap_z(upper),
            ahead_y(below),
            behind_y(below),
            shift(below, lambda h, r, c: (h, r, c ^ 2)),
        )
    )
    pair = jnp.stack([jnp.where(col < 4, upper, twin), jnp.where(col < 4, twin, upper)])
    below_mine = jnp.stack([below, below_one, below_three, below_two])
    one, three, behind, ahead = lax.optimization_barrier(
        (ahead_x(turned), behind_x(turned), ahead_y(pair), behind_y(pair))
    )
    far_first, far_second, two_first, two_second, below_other = lax.optimization_barrier(
        (
            ahead_y(behind[0]),
            behind_y(ahead[1]),
            ahead_x(one[:1536]),
            behind_x(three[1536:]),
            swap_z(below_mine),
        )
    )
    two = jnp.concatenate([two_first, two_second])
    mine = jnp.stack([part[:2048] for part in (turned, one, three, two)])
    odd_mine = jnp.stack([part[2048:] for part in (turned, one, three, two)])
    other = swap_core(mine)
    odd_other = swap_core(odd_mine)
    rows = (pair, behind, ahead, far_first, far_second, below_mine, below_other)
    right_even, left = lower_first(place, rows, mine, other)

    maps = child_maps.reshape(2, 8, 16, 128)
    row_maps = (
        lax.dynamic_index_in_dim(maps, target, 2, keepdims=False).reshape(2, 1, 1024)
        - target * 1024
    )
    col_maps = lax.dynamic_slice_in_dim(maps, 2 * col, 2, 2).transpose(0, 2, 1, 3)
    col_maps = col_maps - (2 * col + jnp.arange(2, dtype=jnp.int32))[None, :, None, None] * 1024
    col_maps = col_maps.reshape(2, 2, 1024, 1)

    def exchange(parcels):
        return lax.all_to_all(parcels.reshape(128, 128, 128), ALL, 0, 0, tiled=True)

    def placed(b, arrived, done=None):
        return place_children(b, place, arrived, row_maps, col_maps, root_front, done)

    parcels = schur_parcels(0, left, right_even, front[0])
    parcels, odd_mine, odd_other = lax.optimization_barrier((parcels, odd_mine, odd_other))
    arrived = exchange(parcels)
    right_odd = lower_right(place, odd_mine, odd_other, mine, other)
    arrived_odd = exchange(schur_parcels(1, left, right_odd, front[0]))
    return placed(1, arrived_odd, placed(0, arrived))


def solution(mesh):
    return jax.shard_map(
        body,
        mesh=mesh,
        in_specs=(
            P("half", "row", "col"),
            P("half", "row", "col"),
            P("half", None, "col"),
            P(),
            P(("half", "row"), "col"),
        ),
        out_specs=P(("half", "row"), "col"),
        check_vma=False,
    )
```

```python
import functools

import jax
import jax.numpy as jnp
from jax import lax
from jax.experimental import pallas as pl
from jax.experimental.pallas import tpu as pltpu
from jax.sharding import PartitionSpec as P

ALL = ("half", "row", "col")
BF16 = jnp.bfloat16
F32 = jnp.float32
VMEM_LIMIT = 58 * 1024 * 1024
ROWS_AXIS = (((1,), (1,)), ((), ()))


def shift(array, move):
    pairs = []
    for half in range(2):
        for row in range(8):
            for col in range(8):
                h, r, c = move(half, row, col)
                pairs.append(((half * 8 + row) * 8 + col, (h * 8 + r) * 8 + c))
    return lax.ppermute(array, ALL, pairs)


def spans(chunk):
    return pl.ds(pl.multiple_of(chunk * 128, 128), 128)


def gather_columns(place_ref, mine_ref, other_ref, out_ref):
    turn, core = place_ref[0], place_ref[1]
    for ref, part in ((mine_ref, core), (other_ref, 1 - core)):
        for index, away in enumerate((0, 3, 1, 2)):
            out_ref[:, spans((turn + away) % 4 * 2 + part)] = ref[index]


def inverse_product(wide_ref, inverse_ref, out_ref):
    for n in range(4):
        reach = (n + 1) * 256
        out_ref[:, n * 256 : reach] = lax.dot_general(
            wide_ref[:, :reach],
            inverse_ref[n * 256 : reach, :reach],
            ROWS_AXIS,
            preferred_element_type=F32,
        ).astype(BF16)


def subtract_product(left_ref, right, front_refs, out_ref):
    product = lax.dot_general(left_ref[...], right, ROWS_AXIS, preferred_element_type=F32)
    for which, front_ref in enumerate(front_refs):
        lanes = slice(which * 128, (which + 1) * 128)
        for k in range(16):
            rows = slice(k * 128, (k + 1) * 128)
            out_ref[k, which] = (
                front_ref[rows, :].astype(F32) - product[rows, lanes]
            ).astype(BF16)


def first_kernel(
    place_ref,
    near_ref,
    behind_ref,
    ahead_ref,
    far_first_ref,
    far_second_ref,
    below_mine_ref,
    below_other_ref,
    mine_ref,
    other_ref,
    inverse_mine_ref,
    inverse_other_ref,
    front_even_ref,
    front_odd_ref,
    out_ref,
    left_out_ref,
    inverse_ref,
    wide_ref,
    right_ref,
    left_ref,
):
    step = pl.program_id(0)
    y, z = place_ref[4], place_ref[3] // 4

    @pl.when(step == 0)
    def _():
        gather_columns(place_ref, inverse_mine_ref, inverse_other_ref, inverse_ref)
        gather_columns(place_ref, mine_ref, other_ref, wide_ref)
        inverse_product(wide_ref, inverse_ref, right_ref)

    @pl.when(step == 1)
    def _():
        for ref, away in ((near_ref, 0), (behind_ref, 3), (ahead_ref, 1)):
            for side in range(2):
                wide_ref[:, spans(side * 4 + (y + away) % 4)] = ref[side]
        wide_ref[:, spans((y + 2) % 4)] = far_first_ref[...]
        wide_ref[:, spans(4 + (y + 2) % 4)] = far_second_ref[...]
        inverse_product(wide_ref, inverse_ref, left_out_ref)
        left_ref[:1024, :] = left_out_ref[...]

    @pl.when(step == 2)
    def _():
        for ref, side in ((below_mine_ref, z), (below_other_ref, 1 - z)):
            for index, away in enumerate((0, 3, 1, 2)):
                wide_ref[:, spans(side * 4 + (y + away) % 4)] = ref[index]
        inverse_product(wide_ref, inverse_ref, left_out_ref)
        left_ref[1024:, :] = left_out_ref[...]

    @pl.when(step > 2)
    def _():
        at = pl.multiple_of((step - 3) * 256, 256)
        subtract_product(
            left_ref, right_ref[pl.ds(at, 256), :], (front_even_ref, front_odd_ref), out_ref
        )


FOUR_PANELS = pl.BlockSpec((4, 1024, 128), lambda i, s: (0, 0, 0))
FOUR_INVERSES = pl.BlockSpec((4, 1024, 128), lambda i, s: (0, 1, 0))
SQUARE = (1024, 1024)


def schur_first(place, rows, mine, other, front):
    def part(i):
        return jnp.clip(i - 1, 0, 1)

    def late(i):
        return jnp.maximum(i - 3, 0)

    pair = pl.BlockSpec((2, 1024, 128), lambda i, s: (0, 0, 0))
    single = pl.BlockSpec((1024, 128), lambda i, s: (0, 0))
    grid_spec = pltpu.PrefetchScalarGridSpec(
        num_scalar_prefetch=1,
        grid=(7,),
        in_specs=[pair] * 3
        + [single] * 2
        + [FOUR_PANELS] * 4
        + [FOUR_INVERSES] * 2
        + [
            pl.BlockSpec((2048, 128), lambda i, s: (0, 4 * late(i))),
            pl.BlockSpec((2048, 128), lambda i, s: (0, 4 * late(i) + 2)),
        ],
        out_specs=[
            pl.BlockSpec((16, 2, 128, 128), lambda i, s: (0, late(i), 0, 0)),
            pl.BlockSpec(SQUARE, lambda i, s: (part(i), 0)),
        ],
        scratch_shapes=[
            pltpu.VMEM(SQUARE, BF16),
            pltpu.VMEM(SQUARE, BF16),
            pltpu.VMEM(SQUARE, BF16),
            pltpu.VMEM((2048, 1024), BF16),
        ],
    )
    return pl.pallas_call(
        first_kernel,
        grid_spec=grid_spec,
        out_shape=[
            jax.ShapeDtypeStruct((16, 8, 128, 128), BF16),
            jax.ShapeDtypeStruct((2048, 1024), BF16),
        ],
        compiler_params=pltpu.CompilerParams(vmem_limit_bytes=VMEM_LIMIT),
        cost_estimate=pl.CostEstimate(
            flops=8 << 30, bytes_accessed=20 << 20, transcendentals=0
        ),
        name="schur_first",
    )(place, *rows, mine, other, mine, other, front, front)


def right_kernel(
    place_ref,
    mine_ref,
    other_ref,
    inverse_mine_ref,
    inverse_other_ref,
    out_ref,
    inverse_ref,
    wide_ref,
):
    gather_columns(place_ref, inverse_mine_ref, inverse_other_ref, inverse_ref)
    gather_columns(place_ref, mine_ref, other_ref, wide_ref)
    inverse_product(wide_ref, inverse_ref, out_ref)


def lower_right(place, mine, other, inverse_mine, inverse_other):
    grid_spec = pltpu.PrefetchScalarGridSpec(
        num_scalar_prefetch=1,
        grid=(1,),
        in_specs=[FOUR_PANELS] * 2 + [FOUR_INVERSES] * 2,
        out_specs=pl.BlockSpec(SQUARE, lambda i, s: (0, 0)),
        scratch_shapes=[pltpu.VMEM(SQUARE, BF16), pltpu.VMEM(SQUARE, BF16)],
    )
    return pl.pallas_call(
        right_kernel,
        grid_spec=grid_spec,
        out_shape=jax.ShapeDtypeStruct(SQUARE, BF16),
        compiler_params=pltpu.CompilerParams(vmem_limit_bytes=VMEM_LIMIT),
        cost_estimate=pl.CostEstimate(
            flops=3 << 29, bytes_accessed=6 << 20, transcendentals=0
        ),
        name="lower_right",
    )(place, mine, other, inverse_mine, inverse_other)


def schur_kernel(left_ref, right_ref, front_even_ref, front_odd_ref, out_ref):
    subtract_product(left_ref, right_ref[...], (front_even_ref, front_odd_ref), out_ref)


def schur_second(left, right, front):
    return pl.pallas_call(
        schur_kernel,
        grid=(4,),
        in_specs=[
            pl.BlockSpec((2048, 1024), lambda i: (0, 0)),
            pl.BlockSpec((256, 1024), lambda i: (i, 0)),
            pl.BlockSpec((2048, 128), lambda i: (0, 4 * i + 1)),
            pl.BlockSpec((2048, 128), lambda i: (0, 4 * i + 3)),
        ],
        out_specs=pl.BlockSpec((16, 2, 128, 128), lambda i: (0, i, 0, 0)),
        out_shape=jax.ShapeDtypeStruct((16, 8, 128, 128), BF16),
        compiler_params=pltpu.CompilerParams(vmem_limit_bytes=VMEM_LIMIT),
        cost_estimate=pl.CostEstimate(
            flops=4 << 30, bytes_accessed=14 << 20, transcendentals=0
        ),
        name="schur_second",
    )(left, right, front, front)


OUT_ROWS = 512


def place_kernel(
    b, place_ref, schur_in_ref, row_map_ref, col_map_ref, base_ref, *refs
):
    out_ref, schur_ref, columns_ref = refs[-3:]
    step = pl.program_id(0)

    @pl.when(step < 2)
    def _():
        for r in range(8):
            for c in range(8):
                schur_ref[r * 128 : (r + 1) * 128, c * 128 : (c + 1) * 128] = schur_in_ref[
                    r * 8 + c
                ]
        ids = lax.broadcasted_iota(jnp.int32, SQUARE, 1)
        pick = jnp.where(col_map_ref[0, 0] == ids, 1.0, 0.0).astype(BF16)
        columns_ref[pl.ds(pl.multiple_of(step * 1024, 1024), 1024), :] = jnp.dot(
            schur_ref[...], pick, preferred_element_type=F32
        ).astype(BF16)

    @pl.when(step >= 2)
    def _():
        first = (step - 2) * OUT_ROWS
        shape = (OUT_ROWS, 1024)
        row_ids = lax.broadcasted_iota(jnp.int32, shape, 0) + first
        total = base_ref[...].astype(F32)
        for child in range(2):
            pick = jnp.where(row_map_ref[child] == row_ids, 1.0, 0.0).astype(BF16)
            total += jnp.dot(
                pick,
                columns_ref[child * 1024 : (child + 1) * 1024, :],
                preferred_element_type=F32,
            )
        rows = row_ids + place_ref[2] * 1024
        cols = lax.broadcasted_iota(jnp.int32, shape, 1) + (
            place_ref[3] * 2048 + b * 1024
        )
        out_ref[...] = jnp.where(rows >= cols, total, 0.0)


def place_children(b, place, arrived, row_maps, col_maps, base, half_done=None):
    grid_spec = pltpu.PrefetchScalarGridSpec(
        num_scalar_prefetch=1,
        grid=(4,),
        in_specs=[
            pl.BlockSpec((64, 128, 128), lambda i, s: (jnp.minimum(i, 1), 0, 0)),
            pl.BlockSpec((2, 1, 1024), lambda i, s: (0, 0, 0)),
            pl.BlockSpec((1, 1, 1024, 1), lambda i, s: (jnp.minimum(i, 1), b, 0, 0)),
            pl.BlockSpec((OUT_ROWS, 1024), lambda i, s: (jnp.maximum(i - 2, 0), b)),
        ]
        + ([] if half_done is None else [pl.BlockSpec(memory_space=pl.ANY)]),
        out_specs=pl.BlockSpec((OUT_ROWS, 1024), lambda i, s: (jnp.maximum(i - 2, 0), b)),
        scratch_shapes=[pltpu.VMEM(SQUARE, BF16), pltpu.VMEM((2048, 1024), BF16)],
    )
    return pl.pallas_call(
        functools.partial(place_kernel, b),
        grid_spec=grid_spec,
        out_shape=jax.ShapeDtypeStruct((1024, 2048), F32),
        input_output_aliases={} if half_done is None else {5: 0},
        compiler_params=pltpu.CompilerParams(vmem_limit_bytes=VMEM_LIMIT),
        cost_estimate=pl.CostEstimate(
            flops=8 << 30, bytes_accessed=10 << 20, transcendentals=0
        ),
        name="place",
    )(
        place,
        arrived,
        row_maps,
        col_maps,
        base,
        *(() if half_done is None else (half_done,)),
    )


def body(front, panel, inverse_block, child_maps, root_front):
    half = lax.axis_index("half")
    row = lax.axis_index("row")
    col = lax.axis_index("col")
    x, core = row // 2, row % 2
    target = half * 8 + row
    place = jnp.stack([(x + 4 - col // 2) % 4, core, target, col, col % 4]).astype(jnp.int32)

    def spread(array):
        return shift(array, lambda h, r, c: (h, (c // 2 + r // 2) % 4 * 2 + c % 2, r))

    def ahead_x(array):
        return shift(array, lambda h, r, c: (h, (r + 2) % 8, c))

    def behind_x(array):
        return shift(array, lambda h, r, c: (h, (r + 6) % 8, c))

    def ahead_y(array):
        return shift(array, lambda h, r, c: (h, r, c // 4 * 4 + (c + 1) % 4))

    def behind_y(array):
        return shift(array, lambda h, r, c: (h, r, c // 4 * 4 + (c + 3) % 4))

    def swap_z(array):
        return shift(array, lambda h, r, c: (h, r, c ^ 4))

    def swap_core(array):
        return shift(array, lambda h, r, c: (h, r ^ 1, c))

    runs = panel[0].reshape(8, 2, 128, 128)
    turned = spread(
        jnp.concatenate(
            [
                runs[:, 0].reshape(1024, 128),
                inverse_block[0],
                runs[:, 1].reshape(1024, 128),
            ]
        )
    )
    upper, below = panel[0, :1024], panel[0, 1024:]
    turned, twin, below_one, below_three, below_two = lax.optimization_barrier(
        (
            turned,
            swap_z(upper),
            ahead_y(below),
            behind_y(below),
            shift(below, lambda h, r, c: (h, r, c ^ 2)),
        )
    )
    pair = jnp.stack([jnp.where(col < 4, upper, twin), jnp.where(col < 4, twin, upper)])
    below_mine = jnp.stack([below, below_one, below_three, below_two])
    one, three, behind, ahead = lax.optimization_barrier(
        (ahead_x(turned), behind_x(turned), ahead_y(pair), behind_y(pair))
    )
    far_first, far_second, two_first, two_second, below_other = lax.optimization_barrier(
        (
            ahead_y(behind[0]),
            behind_y(ahead[1]),
            ahead_x(one[:1536]),
            behind_x(three[1536:]),
            swap_z(below_mine),
        )
    )
    two = jnp.concatenate([two_first, two_second])
    mine = jnp.stack([part[:2048] for part in (turned, one, three, two)])
    odd_mine = jnp.stack([part[2048:] for part in (turned, one, three, two)])
    other = swap_core(mine)
    odd_other = swap_core(odd_mine)
    rows = (pair, behind, ahead, far_first, far_second, below_mine, below_other)
    parcels, left = schur_first(place, rows, mine, other, front[0])

    maps = child_maps.reshape(2, 8, 16, 128)
    row_maps = (
        lax.dynamic_index_in_dim(maps, target, 2, keepdims=False).reshape(2, 1, 1024)
        - target * 1024
    )
    col_maps = lax.dynamic_slice_in_dim(maps, 2 * col, 2, 2).transpose(0, 2, 1, 3)
    col_maps = col_maps - (2 * col + jnp.arange(2, dtype=jnp.int32))[None, :, None, None] * 1024
    col_maps = col_maps.reshape(2, 2, 1024, 1)

    def exchange(parcels):
        return lax.all_to_all(parcels.reshape(128, 128, 128), ALL, 0, 0, tiled=True)

    def placed(b, arrived, done=None):
        return place_children(b, place, arrived, row_maps, col_maps, root_front, done)

    parcels, odd_mine, odd_other = lax.optimization_barrier((parcels, odd_mine, odd_other))
    arrived = exchange(parcels)
    right_odd = lower_right(place, odd_mine, odd_other, mine, other)
    arrived_odd = exchange(schur_second(left, right_odd, front[0]))
    return placed(1, arrived_odd, placed(0, arrived))


def solution(mesh):
    return jax.shard_map(
        body,
        mesh=mesh,
        in_specs=(
            P("half", "row", "col"),
            P("half", "row", "col"),
            P("half", None, "col"),
            P(),
            P(("half", "row"), "col"),
        ),
        out_specs=P(("half", "row"), "col"),
        check_vma=False,
    )
```

```python
import functools

import jax
import jax.numpy as jnp
from jax import lax
from jax.experimental import pallas as pl
from jax.experimental.pallas import tpu as pltpu
from jax.sharding import PartitionSpec as P

ALL = ("half", "row", "col")
BF16 = jnp.bfloat16
F32 = jnp.float32
VMEM_LIMIT = 58 * 1024 * 1024
ROWS_AXIS = (((1,), (1,)), ((), ()))


def shift(array, move):
    pairs = []
    for half in range(2):
        for row in range(8):
            for col in range(8):
                h, r, c = move(half, row, col)
                pairs.append(((half * 8 + row) * 8 + col, (h * 8 + r) * 8 + c))
    return lax.ppermute(array, ALL, pairs)


def spans(chunk):
    return pl.ds(pl.multiple_of(chunk * 128, 128), 128)


def gather_columns(place_ref, mine_ref, other_ref, out_ref):
    turn, core = place_ref[0], place_ref[1]
    for ref, part in ((mine_ref, core), (other_ref, 1 - core)):
        for index, away in enumerate((0, 3, 1, 2)):
            place = (turn + away) % 4
            out_ref[:, spans(place // 2 * 4 + part * 2 + place % 2)] = ref[index]


def inverse_product(wide_ref, inverse_ref, out_ref):
    for n in range(4):
        reach = (n + 1) * 256
        out_ref[:, n * 256 : reach] = lax.dot_general(
            wide_ref[:, :reach],
            inverse_ref[n * 256 : reach, :reach],
            ROWS_AXIS,
            preferred_element_type=F32,
        ).astype(BF16)


def subtract_product(left_ref, right, front_refs, out_ref):
    product = lax.dot_general(left_ref[...], right, ROWS_AXIS, preferred_element_type=F32)
    for which, front_ref in enumerate(front_refs):
        lanes = slice(which * 128, (which + 1) * 128)
        for k in range(16):
            rows = slice(k * 128, (k + 1) * 128)
            out_ref[k, which] = (
                front_ref[rows, :].astype(F32) - product[rows, lanes]
            ).astype(BF16)


def first_kernel(
    place_ref,
    near_ref,
    behind_ref,
    ahead_ref,
    far_first_ref,
    far_second_ref,
    below_mine_ref,
    below_other_ref,
    mine_ref,
    other_ref,
    inverse_mine_ref,
    inverse_other_ref,
    front_even_ref,
    front_odd_ref,
    out_ref,
    left_out_ref,
    inverse_ref,
    wide_ref,
    right_ref,
    left_ref,
):
    step = pl.program_id(0)
    y, z = place_ref[4], place_ref[3] // 4

    @pl.when(step == 0)
    def _():
        gather_columns(place_ref, inverse_mine_ref, inverse_other_ref, inverse_ref)
        gather_columns(place_ref, mine_ref, other_ref, wide_ref)
        inverse_product(wide_ref, inverse_ref, right_ref)

    @pl.when(step == 1)
    def _():
        for ref, away in ((near_ref, 0), (behind_ref, 3), (ahead_ref, 1)):
            for side in range(2):
                wide_ref[:, spans(side * 4 + (y + away) % 4)] = ref[side]
        wide_ref[:, spans((y + 2) % 4)] = far_first_ref[...]
        wide_ref[:, spans(4 + (y + 2) % 4)] = far_second_ref[...]
        inverse_product(wide_ref, inverse_ref, left_out_ref)
        left_ref[:1024, :] = left_out_ref[...]

    @pl.when(step == 2)
    def _():
        for ref, side in ((below_mine_ref, z), (below_other_ref, 1 - z)):
            for index, away in enumerate((0, 3, 1, 2)):
                wide_ref[:, spans(side * 4 + (y + away) % 4)] = ref[index]
        inverse_product(wide_ref, inverse_ref, left_out_ref)
        left_ref[1024:, :] = left_out_ref[...]

    @pl.when(step > 2)
    def _():
        at = pl.multiple_of((step - 3) * 256, 256)
        subtract_product(
            left_ref, right_ref[pl.ds(at, 256), :], (front_even_ref, front_odd_ref), out_ref
        )


FOUR_PANELS = pl.BlockSpec((4, 1024, 128), lambda i, s: (0, 0, 0))
FOUR_INVERSES = pl.BlockSpec((4, 1024, 128), lambda i, s: (0, 1, 0))
SQUARE = (1024, 1024)


def schur_first(place, rows, mine, other, front):
    def part(i):
        return jnp.clip(i - 1, 0, 1)

    def late(i):
        return jnp.maximum(i - 3, 0)

    pair = pl.BlockSpec((2, 1024, 128), lambda i, s: (0, 0, 0))
    single = pl.BlockSpec((1024, 128), lambda i, s: (0, 0))
    grid_spec = pltpu.PrefetchScalarGridSpec(
        num_scalar_prefetch=1,
        grid=(7,),
        in_specs=[pair] * 3
        + [single] * 2
        + [FOUR_PANELS] * 4
        + [FOUR_INVERSES] * 2
        + [
            pl.BlockSpec((2048, 128), lambda i, s: (0, 4 * late(i))),
            pl.BlockSpec((2048, 128), lambda i, s: (0, 4 * late(i) + 2)),
        ],
        out_specs=[
            pl.BlockSpec((16, 2, 128, 128), lambda i, s: (0, late(i), 0, 0)),
            pl.BlockSpec(SQUARE, lambda i, s: (part(i), 0)),
        ],
        scratch_shapes=[
            pltpu.VMEM(SQUARE, BF16),
            pltpu.VMEM(SQUARE, BF16),
            pltpu.VMEM(SQUARE, BF16),
            pltpu.VMEM((2048, 1024), BF16),
        ],
    )
    return pl.pallas_call(
        first_kernel,
        grid_spec=grid_spec,
        out_shape=[
            jax.ShapeDtypeStruct((16, 8, 128, 128), BF16),
            jax.ShapeDtypeStruct((2048, 1024), BF16),
        ],
        compiler_params=pltpu.CompilerParams(vmem_limit_bytes=VMEM_LIMIT),
        cost_estimate=pl.CostEstimate(
            flops=8 << 30, bytes_accessed=20 << 20, transcendentals=0
        ),
        name="schur_first",
    )(place, *rows, mine, other, mine, other, front, front)


def right_kernel(
    place_ref,
    mine_ref,
    other_ref,
    inverse_mine_ref,
    inverse_other_ref,
    out_ref,
    inverse_ref,
    wide_ref,
):
    gather_columns(place_ref, inverse_mine_ref, inverse_other_ref, inverse_ref)
    gather_columns(place_ref, mine_ref, other_ref, wide_ref)
    inverse_product(wide_ref, inverse_ref, out_ref)


def lower_right(place, mine, other, inverse_mine, inverse_other):
    grid_spec = pltpu.PrefetchScalarGridSpec(
        num_scalar_prefetch=1,
        grid=(1,),
        in_specs=[FOUR_PANELS] * 2 + [FOUR_INVERSES] * 2,
        out_specs=pl.BlockSpec(SQUARE, lambda i, s: (0, 0)),
        scratch_shapes=[pltpu.VMEM(SQUARE, BF16), pltpu.VMEM(SQUARE, BF16)],
    )
    return pl.pallas_call(
        right_kernel,
        grid_spec=grid_spec,
        out_shape=jax.ShapeDtypeStruct(SQUARE, BF16),
        compiler_params=pltpu.CompilerParams(vmem_limit_bytes=VMEM_LIMIT),
        cost_estimate=pl.CostEstimate(
            flops=3 << 29, bytes_accessed=6 << 20, transcendentals=0
        ),
        name="lower_right",
    )(place, mine, other, inverse_mine, inverse_other)


def schur_kernel(left_ref, right_ref, front_even_ref, front_odd_ref, out_ref):
    subtract_product(left_ref, right_ref[...], (front_even_ref, front_odd_ref), out_ref)


def schur_second(left, right, front):
    return pl.pallas_call(
        schur_kernel,
        grid=(4,),
        in_specs=[
            pl.BlockSpec((2048, 1024), lambda i: (0, 0)),
            pl.BlockSpec((256, 1024), lambda i: (i, 0)),
            pl.BlockSpec((2048, 128), lambda i: (0, 4 * i + 1)),
            pl.BlockSpec((2048, 128), lambda i: (0, 4 * i + 3)),
        ],
        out_specs=pl.BlockSpec((16, 2, 128, 128), lambda i: (0, i, 0, 0)),
        out_shape=jax.ShapeDtypeStruct((16, 8, 128, 128), BF16),
        compiler_params=pltpu.CompilerParams(vmem_limit_bytes=VMEM_LIMIT),
        cost_estimate=pl.CostEstimate(
            flops=4 << 30, bytes_accessed=14 << 20, transcendentals=0
        ),
        name="schur_second",
    )(left, right, front, front)


OUT_ROWS = 512


def place_kernel(
    b, place_ref, schur_in_ref, row_map_ref, col_map_ref, base_ref, *refs
):
    out_ref, schur_ref, columns_ref = refs[-3:]
    step = pl.program_id(0)

    @pl.when(step < 2)
    def _():
        for r in range(8):
            for c in range(8):
                schur_ref[r * 128 : (r + 1) * 128, c * 128 : (c + 1) * 128] = schur_in_ref[
                    r * 8 + c
                ]
        ids = lax.broadcasted_iota(jnp.int32, SQUARE, 1)
        pick = jnp.where(col_map_ref[0, 0] == ids, 1.0, 0.0).astype(BF16)
        columns_ref[pl.ds(pl.multiple_of(step * 1024, 1024), 1024), :] = jnp.dot(
            schur_ref[...], pick, preferred_element_type=F32
        ).astype(BF16)

    @pl.when(step >= 2)
    def _():
        first = (step - 2) * OUT_ROWS
        shape = (OUT_ROWS, 1024)
        row_ids = lax.broadcasted_iota(jnp.int32, shape, 0) + first
        total = base_ref[...].astype(F32)
        for child in range(2):
            pick = jnp.where(row_map_ref[child] == row_ids, 1.0, 0.0).astype(BF16)
            total += jnp.dot(
                pick,
                columns_ref[child * 1024 : (child + 1) * 1024, :],
                preferred_element_type=F32,
            )
        rows = row_ids + place_ref[2] * 1024
        cols = lax.broadcasted_iota(jnp.int32, shape, 1) + (
            place_ref[3] * 2048 + b * 1024
        )
        out_ref[...] = jnp.where(rows >= cols, total, 0.0)


def place_children(b, place, arrived, row_maps, col_maps, base, half_done=None):
    grid_spec = pltpu.PrefetchScalarGridSpec(
        num_scalar_prefetch=1,
        grid=(4,),
        in_specs=[
            pl.BlockSpec((64, 128, 128), lambda i, s: (jnp.minimum(i, 1), 0, 0)),
            pl.BlockSpec((2, 1, 1024), lambda i, s: (0, 0, 0)),
            pl.BlockSpec((1, 1, 1024, 1), lambda i, s: (jnp.minimum(i, 1), b, 0, 0)),
            pl.BlockSpec((OUT_ROWS, 1024), lambda i, s: (jnp.maximum(i - 2, 0), b)),
        ]
        + ([] if half_done is None else [pl.BlockSpec(memory_space=pl.ANY)]),
        out_specs=pl.BlockSpec((OUT_ROWS, 1024), lambda i, s: (jnp.maximum(i - 2, 0), b)),
        scratch_shapes=[pltpu.VMEM(SQUARE, BF16), pltpu.VMEM((2048, 1024), BF16)],
    )
    return pl.pallas_call(
        functools.partial(place_kernel, b),
        grid_spec=grid_spec,
        out_shape=jax.ShapeDtypeStruct((1024, 2048), F32),
        input_output_aliases={} if half_done is None else {5: 0},
        compiler_params=pltpu.CompilerParams(vmem_limit_bytes=VMEM_LIMIT),
        cost_estimate=pl.CostEstimate(
            flops=8 << 30, bytes_accessed=10 << 20, transcendentals=0
        ),
        name="place",
    )(
        place,
        arrived,
        row_maps,
        col_maps,
        base,
        *(() if half_done is None else (half_done,)),
    )


def body(front, panel, inverse_block, child_maps, root_front):
    half = lax.axis_index("half")
    row = lax.axis_index("row")
    col = lax.axis_index("col")
    x, core = row // 2, row % 2
    target = half * 8 + row
    place = jnp.stack([(x + 4 - col // 2) % 4, core, target, col, col % 4]).astype(jnp.int32)

    def spread(array):
        return shift(
            array, lambda h, r, c: (h, (c // 4 * 2 + c % 2 + r // 2) % 4 * 2 + c % 4 // 2, r)
        )

    def ahead_x(array):
        return shift(array, lambda h, r, c: (h, (r + 2) % 8, c))

    def behind_x(array):
        return shift(array, lambda h, r, c: (h, (r + 6) % 8, c))

    def ahead_y(array):
        return shift(array, lambda h, r, c: (h, r, c // 4 * 4 + (c + 1) % 4))

    def behind_y(array):
        return shift(array, lambda h, r, c: (h, r, c // 4 * 4 + (c + 3) % 4))

    def swap_z(array):
        return shift(array, lambda h, r, c: (h, r, c ^ 4))

    def swap_core(array):
        return shift(array, lambda h, r, c: (h, r ^ 1, c))

    runs = panel[0].reshape(8, 2, 128, 128)
    turned = spread(
        jnp.concatenate(
            [
                runs[:, 0].reshape(1024, 128),
                inverse_block[0],
                runs[:, 1].reshape(1024, 128),
            ]
        )
    )
    upper, below = panel[0, :1024], panel[0, 1024:]
    turned, twin, below_one, below_three, below_two = lax.optimization_barrier(
        (
            turned,
            swap_z(upper),
            ahead_y(below),
            behind_y(below),
            shift(below, lambda h, r, c: (h, r, c ^ 2)),
        )
    )
    pair = jnp.stack([jnp.where(col < 4, upper, twin), jnp.where(col < 4, twin, upper)])
    below_mine = jnp.stack([below, below_one, below_three, below_two])
    one, three, behind, ahead = lax.optimization_barrier(
        (ahead_x(turned), behind_x(turned), ahead_y(pair), behind_y(pair))
    )
    far_first, far_second, two_first, two_second, below_other = lax.optimization_barrier(
        (
            ahead_y(behind[0]),
            behind_y(ahead[1]),
            ahead_x(one[:1536]),
            behind_x(three[1536:]),
            swap_z(below_mine),
        )
    )
    two = jnp.concatenate([two_first, two_second])
    mine = jnp.stack([part[:2048] for part in (turned, one, three, two)])
    odd_mine = jnp.stack([part[2048:] for part in (turned, one, three, two)])
    other = swap_core(mine)
    odd_other = swap_core(odd_mine)
    rows = (pair, behind, ahead, far_first, far_second, below_mine, below_other)
    parcels, left = schur_first(place, rows, mine, other, front[0])

    maps = child_maps.reshape(2, 8, 16, 128)
    row_maps = (
        lax.dynamic_index_in_dim(maps, target, 2, keepdims=False).reshape(2, 1, 1024)
        - target * 1024
    )
    col_maps = lax.dynamic_slice_in_dim(maps, 2 * col, 2, 2).transpose(0, 2, 1, 3)
    col_maps = col_maps - (2 * col + jnp.arange(2, dtype=jnp.int32))[None, :, None, None] * 1024
    col_maps = col_maps.reshape(2, 2, 1024, 1)

    def exchange(parcels):
        return lax.all_to_all(parcels.reshape(128, 128, 128), ALL, 0, 0, tiled=True)

    def placed(b, arrived, done=None):
        return place_children(b, place, arrived, row_maps, col_maps, root_front, done)

    parcels, odd_mine, odd_other = lax.optimization_barrier((parcels, odd_mine, odd_other))
    arrived = exchange(parcels)
    right_odd = lower_right(place, odd_mine, odd_other, mine, other)
    arrived_odd = exchange(schur_second(left, right_odd, front[0]))
    return placed(1, arrived_odd, placed(0, arrived))


def solution(mesh):
    return jax.shard_map(
        body,
        mesh=mesh,
        in_specs=(
            P("half", "row", "col"),
            P("half", "row", "col"),
            P("half", None, "col"),
            P(),
            P(("half", "row"), "col"),
        ),
        out_specs=P(("half", "row"), "col"),
        check_vma=False,
    )
```

```python
import functools

import jax
import jax.numpy as jnp
from jax import lax
from jax.experimental import pallas as pl
from jax.experimental.pallas import tpu as pltpu
from jax.sharding import PartitionSpec as P

ALL = ("half", "row", "col")
BF16 = jnp.bfloat16
F32 = jnp.float32
VMEM_LIMIT = 58 * 1024 * 1024
ROWS_AXIS = (((1,), (1,)), ((), ()))


def shift(array, move):
    pairs = []
    for half in range(2):
        for row in range(8):
            for col in range(8):
                h, r, c = move(half, row, col)
                pairs.append(((half * 8 + row) * 8 + col, (h * 8 + r) * 8 + c))
    return lax.ppermute(array, ALL, pairs)


def spans(chunk):
    return pl.ds(pl.multiple_of(chunk * 128, 128), 128)


def gather_columns(place_ref, mine_ref, other_ref, out_ref):
    turn, core = place_ref[0], place_ref[1]
    for ref, part in ((mine_ref, core), (other_ref, 1 - core)):
        for index, away in enumerate((0, 3, 1, 2)):
            place = (turn + away) % 4
            out_ref[:, spans(place // 2 * 4 + part * 2 + place % 2)] = ref[index]


def inverse_product(wide_ref, inverse_ref, out_ref):
    for n in range(4):
        reach = (n + 1) * 256
        out_ref[:, n * 256 : reach] = lax.dot_general(
            wide_ref[:, :reach],
            inverse_ref[n * 256 : reach, :reach],
            ROWS_AXIS,
            preferred_element_type=F32,
        ).astype(BF16)


def subtract_product(left_ref, right, front_refs, out_ref):
    product = lax.dot_general(left_ref[...], right, ROWS_AXIS, preferred_element_type=F32)
    for which, front_ref in enumerate(front_refs):
        lanes = slice(which * 128, (which + 1) * 128)
        for k in range(16):
            rows = slice(k * 128, (k + 1) * 128)
            out_ref[k, which] = (
                front_ref[rows, :].astype(F32) - product[rows, lanes]
            ).astype(BF16)


def first_kernel(
    place_ref,
    near_ref,
    behind_ref,
    ahead_ref,
    far_first_ref,
    far_second_ref,
    below_mine_ref,
    below_other_ref,
    mine_ref,
    other_ref,
    inverse_mine_ref,
    inverse_other_ref,
    front_even_ref,
    front_odd_ref,
    out_ref,
    left_out_ref,
    inverse_ref,
    wide_ref,
    right_ref,
    left_ref,
):
    step = pl.program_id(0)
    y, z = place_ref[4], place_ref[3] // 4

    @pl.when(step == 0)
    def _():
        gather_columns(place_ref, inverse_mine_ref, inverse_other_ref, inverse_ref)
        gather_columns(place_ref, mine_ref, other_ref, wide_ref)
        inverse_product(wide_ref, inverse_ref, right_ref)

    @pl.when(step == 1)
    def _():
        for ref, away in ((near_ref, 0), (behind_ref, 3), (ahead_ref, 1)):
            for side in range(2):
                wide_ref[:, spans(side * 4 + (y + away) % 4)] = ref[side]
        wide_ref[:, spans((y + 2) % 4)] = far_first_ref[...]
        wide_ref[:, spans(4 + (y + 2) % 4)] = far_second_ref[...]
        inverse_product(wide_ref, inverse_ref, left_out_ref)
        left_ref[:1024, :] = left_out_ref[...]

    @pl.when(step == 2)
    def _():
        for ref, side in ((below_mine_ref, z), (below_other_ref, 1 - z)):
            for index, away in enumerate((0, 3, 1, 2)):
                wide_ref[:, spans(side * 4 + (y + away) % 4)] = ref[index]
        inverse_product(wide_ref, inverse_ref, left_out_ref)
        left_ref[1024:, :] = left_out_ref[...]

    @pl.when(step > 2)
    def _():
        at = pl.multiple_of((step - 3) * 256, 256)
        subtract_product(
            left_ref, right_ref[pl.ds(at, 256), :], (front_even_ref, front_odd_ref), out_ref
        )


FOUR_PANELS = pl.BlockSpec((4, 1024, 128), lambda i, s: (0, 0, 0))
FOUR_INVERSES = pl.BlockSpec((4, 1024, 128), lambda i, s: (0, 1, 0))
SQUARE = (1024, 1024)


def schur_first(place, rows, mine, other, front):
    def part(i):
        return jnp.clip(i - 1, 0, 1)

    def late(i):
        return jnp.maximum(i - 3, 0)

    pair = pl.BlockSpec((2, 1024, 128), lambda i, s: (0, 0, 0))
    single = pl.BlockSpec((1024, 128), lambda i, s: (0, 0))
    grid_spec = pltpu.PrefetchScalarGridSpec(
        num_scalar_prefetch=1,
        grid=(7,),
        in_specs=[pair] * 3
        + [single] * 2
        + [FOUR_PANELS] * 4
        + [FOUR_INVERSES] * 2
        + [
            pl.BlockSpec((2048, 128), lambda i, s: (0, 4 * late(i))),
            pl.BlockSpec((2048, 128), lambda i, s: (0, 4 * late(i) + 2)),
        ],
        out_specs=[
            pl.BlockSpec((16, 2, 128, 128), lambda i, s: (0, late(i), 0, 0)),
            pl.BlockSpec(SQUARE, lambda i, s: (part(i), 0)),
        ],
        scratch_shapes=[
            pltpu.VMEM(SQUARE, BF16),
            pltpu.VMEM(SQUARE, BF16),
            pltpu.VMEM(SQUARE, BF16),
            pltpu.VMEM((2048, 1024), BF16),
        ],
    )
    return pl.pallas_call(
        first_kernel,
        grid_spec=grid_spec,
        out_shape=[
            jax.ShapeDtypeStruct((16, 8, 128, 128), BF16),
            jax.ShapeDtypeStruct((2048, 1024), BF16),
        ],
        compiler_params=pltpu.CompilerParams(vmem_limit_bytes=VMEM_LIMIT),
        cost_estimate=pl.CostEstimate(
            flops=8 << 30, bytes_accessed=20 << 20, transcendentals=0
        ),
        name="schur_first",
    )(place, *rows, mine, other, mine, other, front, front)


def right_kernel(
    place_ref,
    mine_ref,
    other_ref,
    inverse_mine_ref,
    inverse_other_ref,
    out_ref,
    inverse_ref,
    wide_ref,
):
    gather_columns(place_ref, inverse_mine_ref, inverse_other_ref, inverse_ref)
    gather_columns(place_ref, mine_ref, other_ref, wide_ref)
    inverse_product(wide_ref, inverse_ref, out_ref)


def lower_right(place, mine, other, inverse_mine, inverse_other):
    grid_spec = pltpu.PrefetchScalarGridSpec(
        num_scalar_prefetch=1,
        grid=(1,),
        in_specs=[FOUR_PANELS] * 2 + [FOUR_INVERSES] * 2,
        out_specs=pl.BlockSpec(SQUARE, lambda i, s: (0, 0)),
        scratch_shapes=[pltpu.VMEM(SQUARE, BF16), pltpu.VMEM(SQUARE, BF16)],
    )
    return pl.pallas_call(
        right_kernel,
        grid_spec=grid_spec,
        out_shape=jax.ShapeDtypeStruct(SQUARE, BF16),
        compiler_params=pltpu.CompilerParams(vmem_limit_bytes=VMEM_LIMIT),
        cost_estimate=pl.CostEstimate(
            flops=3 << 29, bytes_accessed=6 << 20, transcendentals=0
        ),
        name="lower_right",
    )(place, mine, other, inverse_mine, inverse_other)


def schur_kernel(left_ref, right_ref, front_even_ref, front_odd_ref, out_ref):
    subtract_product(left_ref, right_ref[...], (front_even_ref, front_odd_ref), out_ref)


def schur_second(left, right, front):
    return pl.pallas_call(
        schur_kernel,
        grid=(4,),
        in_specs=[
            pl.BlockSpec((2048, 1024), lambda i: (0, 0)),
            pl.BlockSpec((256, 1024), lambda i: (i, 0)),
            pl.BlockSpec((2048, 128), lambda i: (0, 4 * i + 1)),
            pl.BlockSpec((2048, 128), lambda i: (0, 4 * i + 3)),
        ],
        out_specs=pl.BlockSpec((16, 2, 128, 128), lambda i: (0, i, 0, 0)),
        out_shape=jax.ShapeDtypeStruct((16, 8, 128, 128), BF16),
        compiler_params=pltpu.CompilerParams(vmem_limit_bytes=VMEM_LIMIT),
        cost_estimate=pl.CostEstimate(
            flops=4 << 30, bytes_accessed=14 << 20, transcendentals=0
        ),
        name="schur_second",
    )(left, right, front, front)


OUT_ROWS = 512


def place_kernel(
    b, place_ref, schur_in_ref, row_map_ref, col_map_ref, base_ref, *refs
):
    out_ref, schur_ref, columns_ref = refs[-3:]
    step = pl.program_id(0)

    @pl.when(step < 2)
    def _():
        for r in range(8):
            for c in range(8):
                schur_ref[r * 128 : (r + 1) * 128, c * 128 : (c + 1) * 128] = schur_in_ref[
                    r * 8 + c
                ]
        ids = lax.broadcasted_iota(jnp.int32, SQUARE, 1)
        pick = jnp.where(col_map_ref[0, 0] == ids, 1.0, 0.0).astype(BF16)
        columns_ref[pl.ds(pl.multiple_of(step * 1024, 1024), 1024), :] = jnp.dot(
            schur_ref[...], pick, preferred_element_type=F32
        ).astype(BF16)

    @pl.when(step >= 2)
    def _():
        first = (step - 2) * OUT_ROWS
        shape = (OUT_ROWS, 1024)
        row_ids = lax.broadcasted_iota(jnp.int32, shape, 0) + first
        total = base_ref[...].astype(F32)
        for child in range(2):
            pick = jnp.where(row_map_ref[child] == row_ids, 1.0, 0.0).astype(BF16)
            total += jnp.dot(
                pick,
                columns_ref[child * 1024 : (child + 1) * 1024, :],
                preferred_element_type=F32,
            )
        rows = row_ids + place_ref[2] * 1024
        cols = lax.broadcasted_iota(jnp.int32, shape, 1) + (
            place_ref[3] * 2048 + b * 1024
        )
        out_ref[...] = jnp.where(rows >= cols, total, 0.0)


def place_children(b, place, arrived, row_maps, col_maps, base, half_done=None):
    grid_spec = pltpu.PrefetchScalarGridSpec(
        num_scalar_prefetch=1,
        grid=(4,),
        in_specs=[
            pl.BlockSpec((64, 128, 128), lambda i, s: (jnp.minimum(i, 1), 0, 0)),
            pl.BlockSpec((2, 1, 1024), lambda i, s: (0, 0, 0)),
            pl.BlockSpec((1, 1, 1024, 1), lambda i, s: (jnp.minimum(i, 1), b, 0, 0)),
            pl.BlockSpec((OUT_ROWS, 1024), lambda i, s: (jnp.maximum(i - 2, 0), b)),
        ]
        + ([] if half_done is None else [pl.BlockSpec(memory_space=pl.ANY)]),
        out_specs=pl.BlockSpec((OUT_ROWS, 1024), lambda i, s: (jnp.maximum(i - 2, 0), b)),
        scratch_shapes=[pltpu.VMEM(SQUARE, BF16), pltpu.VMEM((2048, 1024), BF16)],
    )
    return pl.pallas_call(
        functools.partial(place_kernel, b),
        grid_spec=grid_spec,
        out_shape=jax.ShapeDtypeStruct((1024, 2048), F32),
        input_output_aliases={} if half_done is None else {5: 0},
        compiler_params=pltpu.CompilerParams(vmem_limit_bytes=VMEM_LIMIT),
        cost_estimate=pl.CostEstimate(
            flops=8 << 30, bytes_accessed=10 << 20, transcendentals=0
        ),
        name="place",
    )(
        place,
        arrived,
        row_maps,
        col_maps,
        base,
        *(() if half_done is None else (half_done,)),
    )


def body(front, panel, inverse_block, child_maps, root_front):
    half = lax.axis_index("half")
    row = lax.axis_index("row")
    col = lax.axis_index("col")
    x, core = row // 2, row % 2
    target = half * 8 + row
    place = jnp.stack([(x + 4 - col // 2) % 4, core, target, col, col % 4]).astype(jnp.int32)

    def spread(array):
        return shift(
            array, lambda h, r, c: (h, (c // 4 * 2 + c % 2 + r // 2) % 4 * 2 + c % 4 // 2, r)
        )

    def ahead_x(array):
        return shift(array, lambda h, r, c: (h, (r + 2) % 8, c))

    def behind_x(array):
        return shift(array, lambda h, r, c: (h, (r + 6) % 8, c))

    def ahead_y(array):
        return shift(array, lambda h, r, c: (h, r, c // 4 * 4 + (c + 1) % 4))

    def behind_y(array):
        return shift(array, lambda h, r, c: (h, r, c // 4 * 4 + (c + 3) % 4))

    def swap_z(array):
        return shift(array, lambda h, r, c: (h, r, c ^ 4))

    def swap_core(array):
        return shift(array, lambda h, r, c: (h, r ^ 1, c))

    upper, below, whole = lax.optimization_barrier((panel[0, :1024], panel[0, 1024:], panel[0]))
    runs = whole.reshape(8, 2, 128, 128)
    turned = spread(
        jnp.concatenate(
            [
                runs[:, 0].reshape(1024, 128),
                inverse_block[0],
                runs[:, 1].reshape(1024, 128),
            ]
        )
    )
    twin, below_one, below_three, below_two = lax.optimization_barrier(
        (
            swap_z(upper),
            ahead_y(below),
            behind_y(below),
            shift(below, lambda h, r, c: (h, r, c ^ 2)),
        )
    )
    pair = jnp.stack([jnp.where(col < 4, upper, twin), jnp.where(col < 4, twin, upper)])
    below_mine = jnp.stack([below, below_one, below_three, below_two])
    turned, pair, below_mine = lax.optimization_barrier((turned, pair, below_mine))
    one, three, behind, ahead = lax.optimization_barrier(
        (ahead_x(turned), behind_x(turned), ahead_y(pair), behind_y(pair))
    )
    far_first, far_second, two_first, two_second, below_other = lax.optimization_barrier(
        (
            ahead_y(behind[0]),
            behind_y(ahead[1]),
            ahead_x(one[:1536]),
            behind_x(three[1536:]),
            swap_z(below_mine),
        )
    )
    two = jnp.concatenate([two_first, two_second])
    mine = jnp.stack([part[:2048] for part in (turned, one, three, two)])
    odd_mine = jnp.stack([part[2048:] for part in (turned, one, three, two)])
    other = swap_core(mine)
    odd_other = swap_core(odd_mine)
    rows = (pair, behind, ahead, far_first, far_second, below_mine, below_other)
    parcels, left = schur_first(place, rows, mine, other, front[0])

    maps = child_maps.reshape(2, 8, 16, 128)
    row_maps = (
        lax.dynamic_index_in_dim(maps, target, 2, keepdims=False).reshape(2, 1, 1024)
        - target * 1024
    )
    col_maps = lax.dynamic_slice_in_dim(maps, 2 * col, 2, 2).transpose(0, 2, 1, 3)
    col_maps = col_maps - (2 * col + jnp.arange(2, dtype=jnp.int32))[None, :, None, None] * 1024
    col_maps = col_maps.reshape(2, 2, 1024, 1)

    def exchange(parcels):
        return lax.all_to_all(parcels.reshape(128, 128, 128), ALL, 0, 0, tiled=True)

    def placed(b, arrived, done=None):
        return place_children(b, place, arrived, row_maps, col_maps, root_front, done)

    parcels, odd_mine, odd_other = lax.optimization_barrier((parcels, odd_mine, odd_other))
    arrived = exchange(parcels)
    right_odd = lower_right(place, odd_mine, odd_other, mine, other)
    arrived_odd = exchange(schur_second(left, right_odd, front[0]))
    return placed(1, arrived_odd, placed(0, arrived))


def solution(mesh):
    return jax.shard_map(
        body,
        mesh=mesh,
        in_specs=(
            P("half", "row", "col"),
            P("half", "row", "col"),
            P("half", None, "col"),
            P(),
            P(("half", "row"), "col"),
        ),
        out_specs=P(("half", "row"), "col"),
        check_vma=False,
    )
```
